768 devices in a mesh: pair: 32 (over y, x), aux: 24 (over z, core).
Axes of the slice: x: 4, y: 8, z: 12, core: 2. Of those that a mesh axis runs over, the one named last changes fastest.
Arguments:
- amplitudes: bfloat16 [24, 32, 256, 256], P('aux', None, None, 'pair'), may hold values from -4 to 4
- integrals: bfloat16 [24, 32, 2016, 512], P(None, 'pair', 'aux'), may hold values from -1 to 1
- pair_occ: int32 [24, 32, 2], P('aux', 'pair'), may hold values from 0 to 99
- dom_tiles: int32 [24, 32, 2], P('aux', 'pair'), may hold values from 0 to 11, as said below
- dom_mask: int32 [24, 32, 2], P('aux', 'pair'), may hold values 0 or 1
- virt_energy: float32 [1536], replicated, may hold values from 0.3 to 3
- occ_energy: float32 [100], replicated, may hold values from -1.5 to -0.3
Outputs:
- residual: float32 [24, 32, 256, 256], P('aux', 'pair')
The draws below stay inside these ranges and needn't reach their ends.
Inputs may be any that keep to these rules, and one draw needn't show every extreme that they name: `dom_tiles`: the 2 tile ids of one pair are distinct and ascending.
All inputs are finite; a program needn't handle non-finite values. No bound on the sum of `dom_mask` on one device may be relied on, other than what follows from the above.
Results may differ from the reference program's by a relative error of at most 0.0016.
Values may be sent and summed in bfloat16 or wider, within the bound.
No kernel may reach another device: no remote copies, remote signals or barrier semaphores. Data moves between devices by JAX's collectives and lax.ppermute only.
A program may use at most 64 MiB of HBM per device.

```python
import jax
import jax.numpy as jnp
from jax import lax

NOCC = 100
TILE = 128
NT = 12
DT = 2
NAUX = 2016
VIRT = 1536
DOM = 256
GROUPS = 24
GPAIRS = 32


def draw_dom_tiles(key, part):
    key = jax.random.fold_in(key, 7)
    scores = jax.random.randint(key, (GROUPS, GPAIRS, NT), 0, 1 << 20) * NT + jnp.arange(NT, dtype=jnp.int32)
    order = jnp.argsort(scores, axis=-1)[..., :DT]
    return jnp.sort(order, axis=-1).astype(jnp.int32)


def place_ends(result, stream_key, least, high):
    longest = result.shape.index(max(result.shape))
    spots = []
    for shift in (0, 1):
        where = [jax.random.randint(jax.random.fold_in(stream_key, axis), (), 0, length) for axis, length in enumerate(result.shape)]
        where[longest] = (where[longest] + shift) % result.shape[longest]
        spots.append(tuple(where))
    return result.at[spots[0]].set(least).at[spots[1]].set(high)


def spiked(values, own_key, source, target, shards_of, factor):
    def block_of(axis_at):
        return (jnp.arange(values.shape[axis_at]) // (values.shape[axis_at] // shards_of)).reshape((-1,) + (1,) * (values.ndim - 1 - axis_at))

    near = jax.random.permutation(own_key, shards_of)[block_of(target)]
    far = (block_of(target) + shards_of // 2) % shards_of
    return jnp.where((block_of(source) == near) | (block_of(source) == far), factor * values, values)


def levels(rng, shape, cuts, smallest, largest):
    loudness, own = 1.0, jax.random.fold_in(rng, 6)
    for axis_at, shards_of in cuts:
        steps = jnp.exp(jax.random.uniform(jax.random.fold_in(own, axis_at), (shards_of,), jnp.float32, smallest / len(cuts), largest / len(cuts)))
        loudness = loudness * jnp.repeat(steps, shape[axis_at] // shards_of).reshape([-1 if axis == axis_at else 1 for axis in range(len(shape))])
    return loudness


def centred(own_key, shape, scale, most, split=(), kind=jnp.bfloat16):
    entries = scale * jax.random.normal(own_key, shape, jnp.float32)
    if split:
        entries = entries * levels(own_key, shape, split, -0.22, 0.18)
    return jnp.clip(entries, -most, most).astype(kind)


def heavy_noise(key, extent, scale, bound, cuts, heavy, kind=jnp.bfloat16):
    drawn = scale * jax.random.normal(key, extent, jnp.float32)
    if cuts:
        drawn = drawn * levels(key, extent, cuts, -0.22, 0.18)
    return jnp.clip(spiked(drawn, jax.random.fold_in(key, 3), *heavy), -bound, bound).astype(kind)


def setup_inputs(seed: int = 0) -> dict:
    keys = jax.random.split(jax.random.key(seed), 8)
    return {
        "amplitudes": centred(keys[0], (GROUPS, GPAIRS, DOM, DOM), 0.25, 4.0, ((0, 24), (3, 32))),
        "integrals": heavy_noise(keys[1], (GROUPS, GPAIRS, NAUX, 2 * DOM), (2.0 * NAUX ** -0.5), 1.0, ((1, 32), (2, 24)), (2, 0, 24, 2.25)),
        "pair_occ": place_ends(jax.random.randint(keys[2], (GROUPS, GPAIRS, 2), 0, NOCC), jax.random.fold_in(keys[2], 1), 0, NOCC - 1).astype(jnp.int32),
        "dom_tiles": draw_dom_tiles(jax.random.fold_in(keys[7], 71), 0),
        "dom_mask": place_ends((jax.random.randint(keys[4], (GROUPS, GPAIRS, DT), 0, 4) < 3).astype(jnp.int32), jax.random.fold_in(keys[4], 1), 0, 1),
        "virt_energy": jnp.clip(jax.random.uniform(keys[5], (VIRT,), jnp.float32, 0.3, 3.0), 0.3, 3.0),
        "occ_energy": jnp.clip(jax.random.uniform(keys[6], (NOCC,), jnp.float32, -1.5, -0.3), -1.5, -0.3),
    }


def pair_terms(block, amps):
    left = block[:, :DOM]
    right = block[:, DOM:]
    first = jnp.dot(left, amps, preferred_element_type=jnp.float32).astype(jnp.bfloat16)
    second = jnp.dot(left, amps.T, preferred_element_type=jnp.float32).astype(jnp.bfloat16)
    direct = jnp.dot(left.T, right, preferred_element_type=jnp.float32)
    dressed = jnp.dot(left.T, first, preferred_element_type=jnp.float32)
    mirror = jnp.dot(second.T, left, preferred_element_type=jnp.float32)
    return direct - dressed - mirror


def reference(amplitudes, integrals, pair_occ, dom_tiles, dom_mask, virt_energy, occ_energy):
    count = GROUPS * GPAIRS
    flat_int = integrals.reshape(count, NAUX, 2 * DOM)
    flat_amp = amplitudes.reshape(count, DOM, DOM)
    summed = lax.map(lambda pack: pair_terms(pack[0], pack[1]), (flat_int, flat_amp))
    summed = summed.reshape(GROUPS, GPAIRS, DOM, DOM)
    index = (dom_tiles[..., None] * TILE + jnp.arange(TILE, dtype=jnp.int32)).astype(jnp.int32)
    e_dom = virt_energy[index].reshape(GROUPS, GPAIRS, DOM)
    f_sum = occ_energy[pair_occ[..., 0]] + occ_energy[pair_occ[..., 1]]
    delta = (e_dom[..., :, None] + e_dom[..., None, :]) - f_sum[..., None, None]
    keep = jnp.repeat(dom_mask.astype(jnp.float32), TILE, axis=-1)
    outer = keep[..., :, None] * keep[..., None, :]
    return outer * (summed + delta * amplitudes.astype(jnp.float32))
```

```python
import functools

import jax
import jax.numpy as jnp
from jax import lax
from jax.experimental import pallas as pl
from jax.experimental.pallas import tpu as pltpu
from jax.sharding import PartitionSpec as P

TILE = 128
HOPS = 3
ROWS = 6 * TILE + 8
F32 = jnp.float32
BF16 = jnp.bfloat16


def iotas():
    return (
        lax.broadcasted_iota(jnp.int32, (TILE, TILE), 0),
        lax.broadcasted_iota(jnp.int32, (TILE, TILE), 1),
    )


def packed_sum(blocks, store):
    def product(cols):
        total = None
        for block in blocks:
            term = lax.dot_general(
                block[:, : 2 * TILE],
                block[:, cols * TILE : (cols + 1) * TILE],
                (((0,), (0,)), ((), ())),
                preferred_element_type=F32,
            )
            total = term if total is None else total + term
        return total

    row, col = iotas()
    store(0, product(2))
    store(2 * TILE, product(3))
    g0 = product(0)
    g1 = product(1)
    store(4 * TILE, g1[:TILE])
    store(5 * TILE, jnp.where(row <= col, g0[:TILE], g1[TILE:]))
    diag = jnp.sum(jnp.where(row == col, g1[TILE:], 0.0), axis=0, keepdims=True)
    store(6 * TILE, jnp.broadcast_to(diag, (8, TILE)))


def pack_kernel(idx, own, other, *outs):
    for n, out in enumerate(outs):
        out[0] = own[idx[n]]
        out[1] = other[idx[n]]


def pre_kernel(idx, own, other, out):
    def store(at, value):
        out[0, at : at + value.shape[0], :] = value

    packed_sum([own[0], other[0]], store)


def start_kernel(base, half, *rest):
    out = rest[-1]

    def store(at, value):
        out[at : at + value.shape[0], :] = value + base[at : at + value.shape[0], :]

    blocks = [half[0]]
    for ref in rest[:-1]:
        blocks += [ref[0], ref[1]]
    packed_sum(blocks, store)


def final_kernel(occ_at, tiles, mask, occ, virt, pa, pb, pc, amps_t, out):
    row, col = iotas()

    def part(at, rows):
        return pa[at : at + rows, :] + pb[at : at + rows, :] + pc[at : at + rows, :]

    h = jnp.concatenate([part(0, 2 * TILE), part(2 * TILE, 2 * TILE)], axis=1)
    g01 = part(4 * TILE, TILE)
    fold = part(5 * TILE, TILE)
    diag = part(6 * TILE, 8)[:1]
    above = jnp.where(row < col, fold, 0.0)
    below = jnp.where(row > col, fold, 0.0)
    g00 = jnp.where(row <= col, fold, 0.0) + above.T
    g11 = below + below.T + jnp.where(row == col, diag, 0.0)
    g = jnp.concatenate(
        [jnp.concatenate([g00, g01], axis=1), jnp.concatenate([g01.T, g11], axis=1)], axis=0
    )
    tt = amps_t[...]
    total = h
    rest = g
    for _ in range(3):
        piece = rest.astype(BF16)
        rest = rest - piece.astype(F32)
        total = total - lax.dot_general(
            piece, tt, (((1,), (1,)), ((), ())), preferred_element_type=F32
        )
        total = total - lax.dot_general(
            tt, piece, (((0,), (0,)), ((), ())), preferred_element_type=F32
        )
    f_sum = occ[occ_at[0]] + occ[occ_at[1]]
    t = tt.astype(F32).T
    e_row = [virt[pl.ds(tiles[s], 1), :] for s in range(2)]
    e_col = [jnp.sum(jnp.where(row == col, e, 0.0), axis=1, keepdims=True) for e in e_row]
    keep = [mask[s].astype(F32) for s in range(2)]
    for a in range(2):
        for b in range(2):
            at = (slice(a * TILE, (a + 1) * TILE), slice(b * TILE, (b + 1) * TILE))
            delta = (e_col[a] + e_row[b]) - f_sum
            out[at] = (keep[a] * keep[b]) * (total[at] + delta * t[at])


def on_device(chips, amplitudes, integrals, pair_occ, dom_tiles, dom_mask, virt_energy, occ_energy):
    naux, wide = integrals.shape[2:]
    far = chips // 2
    me = lax.axis_index("aux")
    z, c = me // 2, me % 2
    vmem = pl.BlockSpec(memory_space=pltpu.VMEM)
    smem = pl.BlockSpec(memory_space=pltpu.SMEM)

    def sign(core, stream):
        return 1 - 2 * ((core + stream) % 2)

    def permute(x, stream, hops, cross=False):
        pairs = []
        for chip in range(chips):
            for core in range(2):
                to = (chip + sign(core, stream) * hops) % chips
                pairs.append((chip * 2 + core, to * 2 + (core ^ int(cross))))
        return lax.ppermute(x, "aux", pairs)

    def dest(stream, distance):
        return lax.rem(z + sign(c, stream) * distance + chips, chips)

    by_chip = integrals.reshape(chips, 2, naux, wide)
    other = lax.dynamic_index_in_dim(by_chip, 1 - c, 1, keepdims=False)
    own = lax.dynamic_index_in_dim(by_chip, c, 1, keepdims=False)
    across = lax.rem(z + far, chips)
    half = [
        permute(lax.dynamic_slice_in_dim(own, across, 1, 0), 0, far - HOPS),
        permute(lax.dynamic_slice_in_dim(other, across, 1, 0), 0, far - HOPS, cross=True),
    ]
    other = lax.ppermute(other, "aux", [(i, i ^ 1) for i in range(2 * chips)])

    ways = [(s, d) for d in range(far - 1, HOPS, -1) for s in range(2)]
    idx = jnp.stack([dest(s, d) for s, d in ways]).astype(jnp.int32)
    sends = pl.pallas_call(
        pack_kernel,
        in_specs=[smem, vmem, vmem],
        out_specs=[vmem] * len(ways),
        out_shape=[jax.ShapeDtypeStruct((2, naux, wide), BF16)] * len(ways),
        name="pack_rows",
    )(idx, own, other)
    rows = [[], []]
    for (s, d), x in zip(ways, sends):
        rows[s].append(permute(x, s, d - HOPS))

    near = [(s, d) for d in range(HOPS, 0, -1) for s in range(2)] + [(0, 0)]
    idx = jnp.stack([dest(s, d) for s, d in near]).astype(jnp.int32)
    block = pl.BlockSpec((1, naux, wide), lambda n, at: (at[n], 0, 0))
    local = pl.pallas_call(
        pre_kernel,
        grid_spec=pltpu.PrefetchScalarGridSpec(
            num_scalar_prefetch=1,
            grid=(len(near),),
            in_specs=[block, block],
            out_specs=pl.BlockSpec((1, ROWS, TILE), lambda n, at: (n, 0, 0)),
        ),
        out_shape=jax.ShapeDtypeStruct((len(near), ROWS, TILE), F32),
        name="own_sums",
    )(idx, own, other)

    owned = lax.all_to_all(amplitudes, "pair", split_axis=1, concat_axis=3, tiled=True)
    amps_t = jnp.swapaxes(owned[0, 0], 0, 1)

    sums = []
    for s in range(2):
        sums.append(
            pl.pallas_call(
                start_kernel,
                in_specs=[vmem] * (2 + len(rows[s])),
                out_specs=vmem,
                out_shape=jax.ShapeDtypeStruct((ROWS, TILE), F32),
                name="far_sum",
            )(local[s], half[s], *rows[s])
        )
    for hop in range(HOPS):
        for s in range(2):
            sums[s] = permute(sums[s], s, 1)
            if hop < HOPS - 1:
                sums[s] = sums[s] + local[2 * (hop + 1) + s]

    out = pl.pallas_call(
        final_kernel,
        in_specs=[smem] * 4 + [vmem] * 5,
        out_specs=vmem,
        out_shape=jax.ShapeDtypeStruct((2 * TILE, 2 * TILE), F32),
        name="residual",
    )(
        pair_occ.reshape(-1),
        dom_tiles.reshape(-1),
        dom_mask.reshape(-1),
        occ_energy,
        virt_energy.reshape(-1, TILE),
        sums[0],
        sums[1],
        local[2 * HOPS],
        amps_t,
    )
    return out[None, None]


def solution(mesh):
    return jax.shard_map(
        functools.partial(on_device, mesh.shape["aux"] // 2),
        mesh=mesh,
        in_specs=(
            P("aux", None, None, "pair"),
            P(None, "pair", "aux", None),
            P("aux", "pair", None),
            P("aux", "pair", None),
            P("aux", "pair", None),
            P(),
            P(),
        ),
        out_specs=P("aux", "pair", None, None),
        check_vma=False,
    )
```

```python
import functools

import jax
import jax.numpy as jnp
from jax import lax
from jax.experimental import pallas as pl
from jax.experimental.pallas import tpu as pltpu
from jax.sharding import PartitionSpec as P

TILE = 128
HOPS = 3
H_ROWS, G_ROWS = 4 * TILE, 2 * TILE
DIAG = H_ROWS + G_ROWS
H_EXP, G_EXP = DIAG + 1, DIAG + 2
ROWS = DIAG + 16
F32 = jnp.float32
BF16 = jnp.bfloat16
F16 = jnp.float16


def sign(core, stream):
    return 1 - 2 * ((core + stream) % 2)


def here():
    me = lax.axis_index("aux")
    return lax.div(me, 2), lax.rem(me, 2)


def dest(chips, stream, distance):
    z, c = here()
    return lax.rem(z + sign(c, stream) * distance + chips, chips)


def iotas():
    return (
        lax.broadcasted_iota(jnp.int32, (TILE, TILE), 0),
        lax.broadcasted_iota(jnp.int32, (TILE, TILE), 1),
    )


def exponent(*parts):
    top = None
    for part in parts:
        high = jnp.max(jnp.abs(part), axis=0, keepdims=True)
        top = high if top is None else jnp.maximum(top, high)
    top = jnp.max(top, axis=1, keepdims=True)
    power = 14.0 - jnp.floor(jnp.log2(jnp.maximum(top, 1e-30)))
    return jnp.broadcast_to(power, (1, TILE))


def packed_sum(blocks, out):
    total = None
    for block in blocks:
        term = lax.dot_general(
            block[:, : 2 * TILE], block, (((0,), (0,)), ((), ())), preferred_element_type=F32
        )
        total = term if total is None else total + term
    row, col = iotas()
    g00, g01 = total[:TILE, :TILE], total[:TILE, TILE : 2 * TILE]
    g11 = total[TILE:, TILE : 2 * TILE]
    h0, h1 = total[:, 2 * TILE : 3 * TILE], total[:, 3 * TILE :]
    fold = jnp.where(row <= col, g00, g11)
    diag = jnp.sum(jnp.where(row == col, g11, 0.0), axis=0, keepdims=True)
    out[: 2 * TILE] = h0
    out[2 * TILE : H_ROWS] = h1
    out[H_ROWS : H_ROWS + TILE] = g01
    out[H_ROWS + TILE : DIAG] = fold
    lines = lax.broadcasted_iota(jnp.int32, (ROWS - DIAG, TILE), 0)
    rest = jnp.where(lines == 0, diag, 0.0)
    rest = jnp.where(lines == H_EXP - DIAG, exponent(h0, h1), rest)
    out[DIAG:] = jnp.where(lines == G_EXP - DIAG, exponent(g01, fold, diag), rest)


def scales(e_h, e_g):
    row = lax.broadcasted_iota(jnp.int32, (ROWS, TILE), 0)
    return row, jnp.where(row < H_ROWS, jnp.exp2(e_h), jnp.exp2(e_g))


def encode(x, e_h, e_g):
    row, scale = scales(e_h, e_g)
    tail = jnp.where(row == H_EXP, e_h, e_g)
    return jnp.where(row <= DIAG, x * scale, tail).astype(F16)


def decode(x):
    x = x.astype(F32)
    e_h, e_g = x[H_EXP : H_EXP + 1], x[G_EXP : G_EXP + 1]
    return x * scales(-e_h, -e_g)[1], e_h, e_g


def split_kernel(chips, ints, out):
    c = here()[1]
    for chip in range(chips):
        out[chip] = ints[2 * chip + 1 - c]


def pack_kernel(chips, ways, ints, other, *outs):
    c = here()[1]
    for (s, d), out in zip(ways, outs):
        to = dest(chips, s, d)
        out[0] = ints[2 * to + c]
        out[1] = other[to]


def own_kernel(chips, near, ints, other, *outs):
    c = here()[1]
    for (s, d), out in zip(near, outs):
        to = dest(chips, s, d)
        packed_sum([ints[2 * to + c], other[to]], out)


def far_kernel(chips, stream, ints, other, *rest):
    c = here()[1]
    to = dest(chips, stream, HOPS)
    blocks = [ints[2 * to + c], other[to]]
    for ref in rest[:-1]:
        blocks += [ref[0], ref[1]]
    packed_sum(blocks, rest[-1])


def final_kernel(occ_at, tiles, mask, occ, virt, sums, amps_t, out):
    row, col = iotas()
    h = jnp.concatenate([sums[: 2 * TILE], sums[2 * TILE : H_ROWS]], axis=1)
    g01 = sums[H_ROWS : H_ROWS + TILE]
    fold = sums[H_ROWS + TILE : DIAG]
    diag = sums[DIAG : DIAG + 8][:1]
    above = jnp.where(row < col, fold, 0.0)
    below = jnp.where(row > col, fold, 0.0)
    g00 = jnp.where(row <= col, fold, 0.0) + above.T
    g11 = below + below.T + jnp.where(row == col, diag, 0.0)
    g = jnp.concatenate(
        [jnp.concatenate([g00, g01], axis=1), jnp.concatenate([g01.T, g11], axis=1)], axis=0
    )
    tt = amps_t[...]
    total = h
    rest = g
    for _ in range(3):
        piece = rest.astype(BF16)
        rest = rest - piece.astype(F32)
        total = total - lax.dot_general(
            piece, tt, (((1,), (1,)), ((), ())), preferred_element_type=F32
        )
        total = total - lax.dot_general(
            tt, piece, (((0,), (0,)), ((), ())), preferred_element_type=F32
        )
    f_sum = occ[occ_at[0]] + occ[occ_at[1]]
    t = tt.astype(F32).T
    e_row = [virt[pl.ds(tiles[s], 1), :] for s in range(2)]
    e_col = [jnp.sum(jnp.where(row == col, e, 0.0), axis=1, keepdims=True) for e in e_row]
    keep = [mask[s].astype(F32) for s in range(2)]
    for a in range(2):
        for b in range(2):
            at = (slice(a * TILE, (a + 1) * TILE), slice(b * TILE, (b + 1) * TILE))
            delta = (e_col[a] + e_row[b]) - f_sum
            out[at] = (keep[a] * keep[b]) * (total[at] + delta * t[at])


def on_device(chips, amplitudes, integrals, pair_occ, dom_tiles, dom_mask, virt_energy, occ_energy):
    naux, wide = integrals.shape[2:]
    far = chips // 2
    vmem = pl.BlockSpec(memory_space=pltpu.VMEM)
    smem = pl.BlockSpec(memory_space=pltpu.SMEM)

    def call(kernel, n_in, shapes, name, small=0):
        return pl.pallas_call(
            kernel,
            in_specs=[smem] * small + [vmem] * n_in,
            out_specs=[vmem] * len(shapes),
            out_shape=[jax.ShapeDtypeStruct(*s) for s in shapes],
            compiler_params=pltpu.CompilerParams(vmem_limit_bytes=24 << 20),
            name=name,
        )

    def permute(x, stream, hops):
        pairs = []
        for chip in range(chips):
            for core in range(2):
                to = (chip + sign(core, stream) * hops) % chips
                pairs.append((chip * 2 + core, to * 2 + core))
        return lax.ppermute(x, "aux", pairs)

    owned = lax.all_to_all(amplitudes, "pair", split_axis=1, concat_axis=3, tiled=True)

    ints = integrals[:, 0]
    (other,) = call(
        functools.partial(split_kernel, chips), 1, [((chips, naux, wide), BF16)], "split_cores"
    )(ints)
    other = lax.ppermute(other, "aux", [(i, i ^ 1) for i in range(2 * chips)])

    ways = [(s, d) for d in range(far, HOPS, -1) for s in range(2) if d < far or s == 0]
    sends = call(
        functools.partial(pack_kernel, chips, ways),
        2,
        [((2, naux, wide), BF16)] * len(ways),
        "pack_rows",
    )(ints, other)
    rows = [[], []]
    for (s, d), x in zip(ways, sends):
        rows[s].append(permute(x, s, d - HOPS))

    near = [(s, d) for d in range(HOPS - 1, 0, -1) for s in range(2)] + [(0, 0)]
    local = call(
        functools.partial(own_kernel, chips, near),
        2,
        [((ROWS, TILE), F32)] * len(near),
        "own_sums",
    )(ints, other)

    rows[1][-1], owned = lax.optimization_barrier((rows[1][-1], owned))
    amps_t = jnp.swapaxes(owned[0, 0], 0, 1)

    moving = []
    for s in range(2):
        (x,) = call(
            functools.partial(far_kernel, chips, s), 2 + len(rows[s]), [((ROWS, TILE), F32)], "far_sum"
        )(ints, other, *rows[s])
        moving.append(
            permute(encode(x, x[H_EXP : H_EXP + 1], x[G_EXP : G_EXP + 1]), s, 1)
        )
    for hop in range(1, HOPS):
        for s in range(2):
            x, e_h, e_g = decode(moving[s])
            mine = local[2 * (hop - 1) + s]
            e_h = jnp.minimum(e_h, mine[H_EXP : H_EXP + 1]) - 1.0
            e_g = jnp.minimum(e_g, mine[G_EXP : G_EXP + 1]) - 1.0
            x = encode(x + mine, e_h, e_g)
            moving[s] = permute(x, s, 1)
            if s == 0:
                moving[1] = lax.optimization_barrier((moving[1], x))[0]
    sums = decode(moving[0])[0] + decode(moving[1])[0] + local[-1]

    (out,) = call(final_kernel, 3, [((2 * TILE, 2 * TILE), F32)], "residual", 4)(
        pair_occ.reshape(-1),
        dom_tiles.reshape(-1),
        dom_mask.reshape(-1),
        occ_energy,
        virt_energy.reshape(-1, TILE),
        sums,
        amps_t,
    )
    return out[None, None]


def solution(mesh):
    return jax.shard_map(
        functools.partial(on_device, mesh.shape["aux"] // 2),
        mesh=mesh,
        in_specs=(
            P("aux", None, None, "pair"),
            P(None, "pair", "aux", None),
            P("aux", "pair", None),
            P("aux", "pair", None),
            P("aux", "pair", None),
            P(),
            P(),
        ),
        out_specs=P("aux", "pair", None, None),
        check_vma=False,
    )
```

```python
import functools

import jax
import jax.numpy as jnp
from jax import lax
from jax.experimental import pallas as pl
from jax.experimental.pallas import tpu as pltpu
from jax.sharding import PartitionSpec as P

TILE = 128
HOPS = 3
H_ROWS, G_ROWS = 4 * TILE, 2 * TILE
DIAG = H_ROWS + G_ROWS
H_EXP, G_EXP = DIAG + 1, DIAG + 2
ROWS = DIAG + 16
F32 = jnp.float32
BF16 = jnp.bfloat16
F16 = jnp.float16


def here():
    me = lax.axis_index("aux")
    c = lax.rem(me, 2)
    return lax.div(me, 2), c, 1 - 2 * c


def toward(chips, distance):
    z, _, way = here()
    return lax.rem(z + way * distance + chips, chips)


def iotas():
    return (
        lax.broadcasted_iota(jnp.int32, (TILE, TILE), 0),
        lax.broadcasted_iota(jnp.int32, (TILE, TILE), 1),
    )


def exponent(*parts):
    top = None
    for part in parts:
        high = jnp.max(jnp.abs(part), axis=0, keepdims=True)
        top = high if top is None else jnp.maximum(top, high)
    top = jnp.max(top, axis=1, keepdims=True)
    power = 14.0 - jnp.floor(jnp.log2(jnp.maximum(top, 1e-30)))
    return jnp.broadcast_to(power, (1, TILE))


def packed_sum(blocks, out, scaled=False):
    total = None
    for block in blocks:
        term = lax.dot_general(
            block[:, : 2 * TILE], block, (((0,), (0,)), ((), ())), preferred_element_type=F32
        )
        total = term if total is None else total + term
    row, col = iotas()
    g00, g01 = total[:TILE, :TILE], total[:TILE, TILE : 2 * TILE]
    g11 = total[TILE:, TILE : 2 * TILE]
    h0, h1 = total[:, 2 * TILE : 3 * TILE], total[:, 3 * TILE :]
    fold = jnp.where(row <= col, g00, g11)
    diag = jnp.sum(jnp.where(row == col, g11, 0.0), axis=0, keepdims=True)
    e_h, e_g = exponent(h0, h1), exponent(g01, fold, diag)
    if scaled:
        by_h, by_g = jnp.exp2(e_h), jnp.exp2(e_g)
        h0, h1, g01, fold, diag = h0 * by_h, h1 * by_h, g01 * by_g, fold * by_g, diag * by_g
    out[: 2 * TILE] = h0
    out[2 * TILE : H_ROWS] = h1
    out[H_ROWS : H_ROWS + TILE] = g01
    out[H_ROWS + TILE : DIAG] = fold
    lines = lax.broadcasted_iota(jnp.int32, (ROWS - DIAG, TILE), 0)
    rest = jnp.where(lines == 0, diag, 0.0)
    rest = jnp.where(lines == H_EXP - DIAG, e_h, rest)
    out[DIAG:] = jnp.where(lines == G_EXP - DIAG, e_g, rest)


def scales(e_h, e_g):
    row = lax.broadcasted_iota(jnp.int32, (ROWS, TILE), 0)
    return row, jnp.where(row < H_ROWS, jnp.exp2(e_h), jnp.exp2(e_g))


def encode(x, e_h, e_g):
    row, scale = scales(e_h, e_g)
    tail = jnp.where(row == H_EXP, e_h, e_g)
    return jnp.where(row <= DIAG, x * scale, tail).astype(F16)


def decode(x):
    x = x.astype(F32)
    e_h, e_g = x[H_EXP : H_EXP + 1], x[G_EXP : G_EXP + 1]
    return x * scales(-e_h, -e_g)[1], e_h, e_g


def split_kernel(chips, ints, out):
    z, c, _ = here()
    near = chips // 2 - 1
    for d in range(1, near + 1):
        to = toward(chips, -d)
        out[2 * d - 2] = ints[2 * to + 1 - c]
        out[2 * d - 1] = ints[2 * to + c]
    out[2 * near] = ints[2 * lax.rem(z + near + 1, chips) + 1 - c]
    out[2 * near + 1] = ints[2 * z + 1 - c]


def chip_rows(chips, ints, other, distance, mine):
    c = here()[1]
    near = chips // 2 - 1
    if distance == 0:
        at = 2 * near + 1
    elif distance > near:
        at = 2 * near
    else:
        at = 2 * distance - 1 - int(mine)
    return [ints[2 * toward(chips, distance) + (c if mine else 1 - c)], other[at]]


def pack_kernel(chips, distances, ints, other, *outs):
    for d, out in zip(distances, outs):
        rows = chip_rows(chips, ints, other, d, True)
        if d < chips // 2:
            rows += chip_rows(chips, ints, other, d, False)
        for n, row in enumerate(rows):
            out[n] = row


def own_kernel(chips, wanted, ints, other, *outs):
    for (d, mine), out in zip(wanted, outs):
        packed_sum(chip_rows(chips, ints, other, d, mine), out)


def far_kernel(chips, mine, ints, other, *rest):
    blocks = chip_rows(chips, ints, other, HOPS, mine)
    for ref in rest[:-1]:
        at = 0 if mine else 2
        blocks += [ref[at], ref[at + 1]]
    packed_sum(blocks, rest[-1], scaled=True)


def final_kernel(occ_at, tiles, mask, occ, virt, sums, amps_t, out):
    row, col = iotas()
    h = jnp.concatenate([sums[: 2 * TILE], sums[2 * TILE : H_ROWS]], axis=1)
    g01 = sums[H_ROWS : H_ROWS + TILE]
    fold = sums[H_ROWS + TILE : DIAG]
    diag = sums[DIAG : DIAG + 8][:1]
    above = jnp.where(row < col, fold, 0.0)
    below = jnp.where(row > col, fold, 0.0)
    g00 = jnp.where(row <= col, fold, 0.0) + above.T
    g11 = below + below.T + jnp.where(row == col, diag, 0.0)
    g = jnp.concatenate(
        [jnp.concatenate([g00, g01], axis=1), jnp.concatenate([g01.T, g11], axis=1)], axis=0
    )
    tt = amps_t[...]
    total = h
    rest = g
    for _ in range(3):
        piece = rest.astype(BF16)
        rest = rest - piece.astype(F32)
        total = total - lax.dot_general(
            piece, tt, (((1,), (1,)), ((), ())), preferred_element_type=F32
        )
        total = total - lax.dot_general(
            tt, piece, (((0,), (0,)), ((), ())), preferred_element_type=F32
        )
    f_sum = occ[occ_at[0]] + occ[occ_at[1]]
    t = tt.astype(F32).T
    e_row = [virt[pl.ds(tiles[s], 1), :] for s in range(2)]
    e_col = [jnp.sum(jnp.where(row == col, e, 0.0), axis=1, keepdims=True) for e in e_row]
    keep = [mask[s].astype(F32) for s in range(2)]
    for a in range(2):
        for b in range(2):
            at = (slice(a * TILE, (a + 1) * TILE), slice(b * TILE, (b + 1) * TILE))
            delta = (e_col[a] + e_row[b]) - f_sum
            out[at] = (keep[a] * keep[b]) * (total[at] + delta * t[at])


def on_device(chips, amplitudes, integrals, pair_occ, dom_tiles, dom_mask, virt_energy, occ_energy):
    naux, wide = integrals.shape[2:]
    far = chips // 2
    vmem = pl.BlockSpec(memory_space=pltpu.VMEM)
    smem = pl.BlockSpec(memory_space=pltpu.SMEM)

    def call(kernel, n_in, shapes, name, small=0):
        return pl.pallas_call(
            kernel,
            in_specs=[smem] * small + [vmem] * n_in,
            out_specs=[vmem] * len(shapes),
            out_shape=[jax.ShapeDtypeStruct(*s) for s in shapes],
            compiler_params=pltpu.CompilerParams(vmem_limit_bytes=24 << 20),
            name=name,
        )

    def permute(x, hops, cross=False):
        pairs = []
        for chip in range(chips):
            for core in range(2):
                to = (chip + (1 - 2 * core) * hops) % chips
                pairs.append((chip * 2 + core, to * 2 + (core ^ int(cross))))
        return lax.ppermute(x, "aux", pairs)

    def summed(wanted, other):
        return call(
            functools.partial(own_kernel, chips, wanted),
            2,
            [((ROWS, TILE), F32)] * len(wanted),
            "own_sums",
        )(ints, other)

    owned = lax.all_to_all(amplitudes, "pair", split_axis=1, concat_axis=3, tiled=True)

    ints = integrals[:, 0]
    (other,) = call(
        functools.partial(split_kernel, chips), 1, [((chips, naux, wide), BF16)], "split_cores"
    )(ints)
    other = lax.ppermute(other, "aux", [(i, i ^ 1) for i in range(2 * chips)])

    distances = list(range(far, HOPS, -1))
    sends = call(
        functools.partial(pack_kernel, chips, distances),
        2,
        [((2 if d == far else 4, naux, wide), BF16) for d in distances],
        "pack_rows",
    )(ints, other)
    rows = [permute(x, d - HOPS) for d, x in zip(distances, sends)]
    rows[-1], owned = lax.optimization_barrier((rows[-1], owned))
    amps_t = jnp.swapaxes(owned[0, 0], 0, 1)

    moving = []
    for mine in (True, False):
        (x,) = call(
            functools.partial(far_kernel, chips, mine),
            2 + len(rows[0 if mine else 1 :]),
            [((ROWS, TILE), F32)],
            "far_sum",
        )(ints, other, *rows[0 if mine else 1 :])
        x = x.astype(F16)
        moving.append(permute(x, 1, HOPS == 1 and not mine))
    for d in range(HOPS - 1, 0, -1):
        local = summed([(d, True), (d, False)], lax.optimization_barrier((other, x))[0])
        for n in range(2):
            x, e_h, e_g = decode(moving[n])
            own = local[n]
            e_h = jnp.minimum(e_h, own[H_EXP : H_EXP + 1]) - 1.0
            e_g = jnp.minimum(e_g, own[G_EXP : G_EXP + 1]) - 1.0
            x = encode(x + own, e_h, e_g)
            moving[n] = permute(x, 1, d == 1 and n == 1)
            if n == 0:
                moving[1] = lax.optimization_barrier((moving[1], x))[0]
    (local,) = summed([(0, True)], lax.optimization_barrier((other, x))[0])
    sums = decode(moving[0])[0] + decode(moving[1])[0] + local

    (out,) = call(final_kernel, 3, [((2 * TILE, 2 * TILE), F32)], "residual", 4)(
        pair_occ.reshape(-1),
        dom_tiles.reshape(-1),
        dom_mask.reshape(-1),
        occ_energy,
        virt_energy.reshape(-1, TILE),
        sums,
        amps_t,
    )
    return out[None, None]


def solution(mesh):
    return jax.shard_map(
        functools.partial(on_device, mesh.shape["aux"] // 2),
        mesh=mesh,
        in_specs=(
            P("aux", None, None, "pair"),
            P(None, "pair", "aux", None),
            P("aux", "pair", None),
            P("aux", "pair", None),
            P("aux", "pair", None),
            P(),
            P(),
        ),
        out_specs=P("aux", "pair", None, None),
        check_vma=False,
    )
```

```python
import functools

import jax
import jax.numpy as jnp
from jax import lax
from jax.experimental import pallas as pl
from jax.experimental.pallas import tpu as pltpu
from jax.sharding import PartitionSpec as P

TILE = 128
FIRST, SECOND = 4, 2
H_ROWS, G_ROWS = 4 * TILE, 2 * TILE
DIAG = H_ROWS + G_ROWS
H_EXP, G_EXP = DIAG + 1, DIAG + 2
ROWS = DIAG + 16
F32 = jnp.float32
BF16 = jnp.bfloat16
F16 = jnp.float16


def here():
    me = lax.axis_index("aux")
    c = lax.rem(me, 2)
    return lax.div(me, 2), c, 1 - 2 * c


def toward(chips, distance):
    z, _, way = here()
    return lax.rem(z + way * distance + chips, chips)


def iotas():
    return (
        lax.broadcasted_iota(jnp.int32, (TILE, TILE), 0),
        lax.broadcasted_iota(jnp.int32, (TILE, TILE), 1),
    )


def exponent(*parts):
    top = None
    for part in parts:
        high = jnp.max(jnp.abs(part), axis=0, keepdims=True)
        top = high if top is None else jnp.maximum(top, high)
    top = jnp.max(top, axis=1, keepdims=True)
    power = 14.0 - jnp.floor(jnp.log2(jnp.maximum(top, 1e-30)))
    return jnp.broadcast_to(power, (1, TILE))


def packed_sum(blocks, out, scaled=False):
    total = None
    for block in blocks:
        term = lax.dot_general(
            block[:, : 2 * TILE], block, (((0,), (0,)), ((), ())), preferred_element_type=F32
        )
        total = term if total is None else total + term
    row, col = iotas()
    g00, g01 = total[:TILE, :TILE], total[:TILE, TILE : 2 * TILE]
    g11 = total[TILE:, TILE : 2 * TILE]
    h0, h1 = total[:, 2 * TILE : 3 * TILE], total[:, 3 * TILE :]
    fold = jnp.where(row <= col, g00, g11)
    diag = jnp.sum(jnp.where(row == col, g11, 0.0), axis=0, keepdims=True)
    e_h, e_g = exponent(h0, h1), exponent(g01, fold, diag)
    if scaled:
        by_h, by_g = jnp.exp2(e_h), jnp.exp2(e_g)
        h0, h1, g01, fold, diag = h0 * by_h, h1 * by_h, g01 * by_g, fold * by_g, diag * by_g
    out[: 2 * TILE] = h0
    out[2 * TILE : H_ROWS] = h1
    out[H_ROWS : H_ROWS + TILE] = g01
    out[H_ROWS + TILE : DIAG] = fold
    lines = lax.broadcasted_iota(jnp.int32, (ROWS - DIAG, TILE), 0)
    rest = jnp.where(lines == 0, diag, 0.0)
    rest = jnp.where(lines == H_EXP - DIAG, e_h, rest)
    out[DIAG:] = jnp.where(lines == G_EXP - DIAG, e_g, rest)


def scales(e_h, e_g):
    row = lax.broadcasted_iota(jnp.int32, (1, ROWS, TILE), 1)
    return row, jnp.where(row < H_ROWS, jnp.exp2(e_h), jnp.exp2(e_g))


def exponents(x):
    return x[:, H_EXP : H_EXP + 1], x[:, G_EXP : G_EXP + 1]


def decode(x):
    x = x.astype(F32)
    e_h, e_g = exponents(x)
    return x * scales(-e_h, -e_g)[1], e_h, e_g


def add_on(x, own):
    x, e_h, e_g = decode(x)
    own_h, own_g = exponents(own)
    e_h, e_g = jnp.minimum(e_h, own_h) - 1.0, jnp.minimum(e_g, own_g) - 1.0
    row, scale = scales(e_h, e_g)
    tail = jnp.where(row == H_EXP, e_h, e_g)
    return jnp.where(row <= DIAG, (x + own) * scale, tail).astype(F16)


def split_kernel(chips, ints, out):
    z, c, _ = here()
    near = chips // 2 - 1
    for d in range(1, near + 1):
        to = toward(chips, -d)
        out[2 * d - 2] = ints[2 * to + 1 - c]
        out[2 * d - 1] = ints[2 * to + c]
    out[2 * near] = ints[2 * lax.rem(z + near + 1, chips) + 1 - c]
    out[2 * near + 1] = ints[2 * z + 1 - c]


def chip_rows(chips, ints, other, distance, mine):
    c = here()[1]
    near = chips // 2 - 1
    if distance == 0:
        at = 2 * near + 1
    elif distance > near:
        at = 2 * near
    else:
        at = 2 * distance - 1 - int(mine)
    return [ints[2 * toward(chips, distance) + (c if mine else 1 - c)], other[at]]


def pack_kernel(chips, wanted, ints, other, *outs):
    for group, out in zip(wanted, outs):
        for n, row in enumerate(sum((chip_rows(chips, ints, other, *w) for w in group), [])):
            out[n] = row


def stop_kernel(chips, stop, owners, picks, scaled, ints, other, *rest):
    received, out = rest[:-1], rest[-1]
    for n, mine in enumerate(owners):
        blocks = chip_rows(chips, ints, other, stop, mine)
        for at, ref in picks:
            if at[n] is not None:
                blocks += [received[ref][at[n]], received[ref][at[n] + 1]]
        packed_sum(blocks, out.at[n], scaled)


def final_kernel(occ_at, tiles, mask, occ, virt, sums, amps_t, out):
    row, col = iotas()
    h = jnp.concatenate([sums[: 2 * TILE], sums[2 * TILE : H_ROWS]], axis=1)
    g01 = sums[H_ROWS : H_ROWS + TILE]
    fold = sums[H_ROWS + TILE : DIAG]
    diag = sums[DIAG : DIAG + 8][:1]
    above = jnp.where(row < col, fold, 0.0)
    below = jnp.where(row > col, fold, 0.0)
    g00 = jnp.where(row <= col, fold, 0.0) + above.T
    g11 = below + below.T + jnp.where(row == col, diag, 0.0)
    g = jnp.concatenate(
        [jnp.concatenate([g00, g01], axis=1), jnp.concatenate([g01.T, g11], axis=1)], axis=0
    )
    tt = amps_t[...]
    total = h
    rest = g
    for _ in range(3):
        piece = rest.astype(BF16)
        rest = rest - piece.astype(F32)
        total = total - lax.dot_general(
            piece, tt, (((1,), (1,)), ((), ())), preferred_element_type=F32
        )
        total = total - lax.dot_general(
            tt, piece, (((0,), (0,)), ((), ())), preferred_element_type=F32
        )
    f_sum = occ[occ_at[0]] + occ[occ_at[1]]
    t = tt.astype(F32).T
    e_row = [virt[pl.ds(tiles[s], 1), :] for s in range(2)]
    e_col = [jnp.sum(jnp.where(row == col, e, 0.0), axis=1, keepdims=True) for e in e_row]
    keep = [mask[s].astype(F32) for s in range(2)]
    for a in range(2):
        for b in range(2):
            at = (slice(a * TILE, (a + 1) * TILE), slice(b * TILE, (b + 1) * TILE))
            delta = (e_col[a] + e_row[b]) - f_sum
            out[at] = (keep[a] * keep[b]) * (total[at] + delta * t[at])


def on_device(chips, amplitudes, integrals, pair_occ, dom_tiles, dom_mask, virt_energy, occ_energy):
    naux, wide = integrals.shape[2:]
    far = chips // 2
    vmem = pl.BlockSpec(memory_space=pltpu.VMEM)
    smem = pl.BlockSpec(memory_space=pltpu.SMEM)

    def call(kernel, n_in, shapes, name, small=0):
        return pl.pallas_call(
            kernel,
            in_specs=[smem] * small + [vmem] * n_in,
            out_specs=[vmem] * len(shapes),
            out_shape=[jax.ShapeDtypeStruct(*s) for s in shapes],
            compiler_params=pltpu.CompilerParams(vmem_limit_bytes=8 << 20),
            name=name,
        )

    def permute(x, hops, cross=False):
        pairs = []
        for chip in range(chips):
            for core in range(2):
                to = (chip + (1 - 2 * core) * hops) % chips
                pairs.append((chip * 2 + core, to * 2 + (core ^ int(cross))))
        return lax.ppermute(x, "aux", pairs)

    def pack(wanted, other):
        return call(
            functools.partial(pack_kernel, chips, wanted),
            2,
            [((2 * len(group), naux, wide), BF16) for group in wanted],
            "pack_rows",
        )(ints, other)

    def stop_sums(stop, owners, picks, scaled, other, received):
        return call(
            functools.partial(stop_kernel, chips, stop, owners, picks, scaled),
            2 + len(received),
            [((len(owners), ROWS, TILE), F32)],
            "stop_sums",
        )(ints, other, *received)[0]

    def pairs_at(d):
        return [(d, True)] if d == far else [(d, True), (d, False)]

    owned = lax.all_gather(jnp.swapaxes(amplitudes[0], 1, 2), "pair")
    owned = lax.dynamic_index_in_dim(owned, lax.axis_index("pair"), 1, keepdims=False)

    ints = integrals[:, 0]
    (other,) = call(
        functools.partial(split_kernel, chips), 1, [((chips, naux, wide), BF16)], "split_cores"
    )(ints)
    other = lax.ppermute(other, "aux", [(i, i ^ 1) for i in range(2 * chips)])

    to_first = list(range(far, FIRST, -1))
    to_second = list(range(FIRST - 1, SECOND, -1))
    to_owner = list(range(SECOND - 1, 0, -1))
    sends = pack([pairs_at(d) for d in to_first], other)
    first_rows = [permute(x, d - FIRST) for d, x in zip(to_first, sends)]
    gate = lax.optimization_barrier((other, *sends))[0]
    sends = pack([pairs_at(d) for d in to_second], gate)
    second_rows = [permute(x, d - SECOND) for d, x in zip(to_second, sends)]

    picks = [((0, None) if d == far else (0, 2), at) for at, d in enumerate(to_first)]
    x = stop_sums(FIRST, (True, False), picks, True, other, first_rows).astype(F16)
    x, *second_rows = lax.optimization_barrier((x, *second_rows))
    moving = permute(x, FIRST - SECOND)

    gate = lax.optimization_barrier((other, x))[0]
    sends = pack([[(d, mine)] for d in to_owner for mine in (True, False)], gate)
    ways = [(d, n == 1) for d in to_owner for n in range(2)]
    owner_rows = [permute(x, *way) for way, x in zip(ways, sends)]
    picks = [((0, 2), at) for at in range(len(to_second))]
    local = stop_sums(SECOND, (True, False), picks, False, gate, second_rows)
    last = [add_on(moving[n : n + 1], local[n : n + 1])[0] for n in range(2)]
    *last, owner_rows = lax.optimization_barrier((*last, owner_rows))
    moving = [permute(last[n], SECOND, n == 1) for n in range(2)]

    gate = lax.optimization_barrier((other, last[1]))[0]
    picks = [((0,), at) for at in range(len(owner_rows))]
    local = stop_sums(0, (True,), picks, False, gate, owner_rows)
    sums = (decode(moving[0][None])[0] + decode(moving[1][None])[0] + local)[0]
    amps_t = owned.reshape(2 * TILE, 2 * TILE)

    (out,) = call(final_kernel, 3, [((2 * TILE, 2 * TILE), F32)], "residual", 4)(
        pair_occ.reshape(-1),
        dom_tiles.reshape(-1),
        dom_mask.reshape(-1),
        occ_energy,
        virt_energy.reshape(-1, TILE),
        sums,
        amps_t,
    )
    return out[None, None]


def solution(mesh):
    return jax.shard_map(
        functools.partial(on_device, mesh.shape["aux"] // 2),
        mesh=mesh,
        in_specs=(
            P("aux", None, None, "pair"),
            P(None, "pair", "aux", None),
            P("aux", "pair", None),
            P("aux", "pair", None),
            P("aux", "pair", None),
            P(),
            P(),
        ),
        out_specs=P("aux", "pair", None, None),
        check_vma=False,
    )
```

```python
import functools

import jax
import jax.numpy as jnp
from jax import lax
from jax.experimental import pallas as pl
from jax.experimental.pallas import tpu as pltpu
from jax.sharding import PartitionSpec as P

TILE = 128
FIRST, SECOND = 4, 2
H_ROWS, G_ROWS = 4 * TILE, 2 * TILE
DIAG = H_ROWS + G_ROWS
H_EXP, G_EXP = DIAG + 1, DIAG + 2
ROWS = DIAG + 16
F32 = jnp.float32
BF16 = jnp.bfloat16
F16 = jnp.float16


def here():
    me = lax.axis_index("aux")
    c = lax.rem(me, 2)
    return lax.div(me, 2), c, 1 - 2 * c


def toward(chips, distance):
    z, _, way = here()
    return lax.rem(z + way * distance + chips, chips)


def iotas():
    return (
        lax.broadcasted_iota(jnp.int32, (TILE, TILE), 0),
        lax.broadcasted_iota(jnp.int32, (TILE, TILE), 1),
    )


def exponent(*parts):
    top = None
    for part in parts:
        high = jnp.max(jnp.abs(part), axis=0, keepdims=True)
        top = high if top is None else jnp.maximum(top, high)
    top = jnp.max(top, axis=1, keepdims=True)
    power = 14.0 - jnp.floor(jnp.log2(jnp.maximum(top, 1e-30)))
    return jnp.broadcast_to(power, (1, TILE))


def packed_sum(blocks, out, scaled=False):
    total = None
    for block in blocks:
        term = lax.dot_general(
            block[:, : 2 * TILE], block, (((0,), (0,)), ((), ())), preferred_element_type=F32
        )
        total = term if total is None else total + term
    row, col = iotas()
    g00, g01 = total[:TILE, :TILE], total[:TILE, TILE : 2 * TILE]
    g11 = total[TILE:, TILE : 2 * TILE]
    h0, h1 = total[:, 2 * TILE : 3 * TILE], total[:, 3 * TILE :]
    fold = jnp.where(row <= col, g00, g11)
    diag = jnp.sum(jnp.where(row == col, g11, 0.0), axis=0, keepdims=True)
    e_h, e_g = exponent(h0, h1), exponent(g01, fold, diag)
    if scaled:
        by_h, by_g = jnp.exp2(e_h), jnp.exp2(e_g)
        h0, h1, g01, fold, diag = h0 * by_h, h1 * by_h, g01 * by_g, fold * by_g, diag * by_g
    out[: 2 * TILE] = h0
    out[2 * TILE : H_ROWS] = h1
    out[H_ROWS : H_ROWS + TILE] = g01
    out[H_ROWS + TILE : DIAG] = fold
    lines = lax.broadcasted_iota(jnp.int32, (ROWS - DIAG, TILE), 0)
    rest = jnp.where(lines == 0, diag, 0.0)
    rest = jnp.where(lines == H_EXP - DIAG, e_h, rest)
    out[DIAG:] = jnp.where(lines == G_EXP - DIAG, e_g, rest)


def scales(e_h, e_g):
    row = lax.broadcasted_iota(jnp.int32, (1, ROWS, TILE), 1)
    return row, jnp.where(row < H_ROWS, jnp.exp2(e_h), jnp.exp2(e_g))


def exponents(x):
    return x[:, H_EXP : H_EXP + 1], x[:, G_EXP : G_EXP + 1]


def decode(x):
    x = x.astype(F32)
    e_h, e_g = exponents(x)
    return x * scales(-e_h, -e_g)[1], e_h, e_g


def add_on(x, own):
    x, e_h, e_g = decode(x)
    own_h, own_g = exponents(own)
    e_h, e_g = jnp.minimum(e_h, own_h) - 1.0, jnp.minimum(e_g, own_g) - 1.0
    row, scale = scales(e_h, e_g)
    tail = jnp.where(row == H_EXP, e_h, e_g)
    return jnp.where(row <= DIAG, (x + own) * scale, tail).astype(F16)


def split_kernel(chips, ints, out):
    z, c, _ = here()
    near = chips // 2 - 1
    for d in range(1, near + 1):
        to = toward(chips, -d)
        out[2 * d - 2] = ints[2 * to + 1 - c]
        out[2 * d - 1] = ints[2 * to + c]
    out[2 * near] = ints[2 * lax.rem(z + near + 1, chips) + 1 - c]
    out[2 * near + 1] = ints[2 * z + 1 - c]


def chip_rows(chips, ints, other, distance, mine):
    c = here()[1]
    near = chips // 2 - 1
    if distance == 0:
        at = 2 * near + 1
    elif distance > near:
        at = 2 * near
    else:
        at = 2 * distance - 1 - int(mine)
    return [ints[2 * toward(chips, distance) + (c if mine else 1 - c)], other[at]]


def pack_kernel(chips, wanted, ints, other, *outs):
    for group, out in zip(wanted, outs):
        for n, row in enumerate(sum((chip_rows(chips, ints, other, *w) for w in group), [])):
            out[n] = row


def stop_kernel(chips, stop, owners, picks, scaled, ints, other, *rest):
    received, out = rest[:-1], rest[-1]
    for n, mine in enumerate(owners):
        blocks = chip_rows(chips, ints, other, stop, mine)
        for at, ref in picks:
            if at[n] is not None:
                blocks += [received[ref][at[n]], received[ref][at[n] + 1]]
        packed_sum(blocks, out.at[n], scaled)


def final_kernel(occ_at, tiles, mask, occ, virt, sums, amps_t, out):
    row, col = iotas()
    h = jnp.concatenate([sums[: 2 * TILE], sums[2 * TILE : H_ROWS]], axis=1)
    g01 = sums[H_ROWS : H_ROWS + TILE]
    fold = sums[H_ROWS + TILE : DIAG]
    diag = sums[DIAG : DIAG + 8][:1]
    above = jnp.where(row < col, fold, 0.0)
    below = jnp.where(row > col, fold, 0.0)
    g00 = jnp.where(row <= col, fold, 0.0) + above.T
    g11 = below + below.T + jnp.where(row == col, diag, 0.0)
    g = jnp.concatenate(
        [jnp.concatenate([g00, g01], axis=1), jnp.concatenate([g01.T, g11], axis=1)], axis=0
    )
    tt = amps_t[...]
    total = h
    rest = g
    for _ in range(3):
        piece = rest.astype(BF16)
        rest = rest - piece.astype(F32)
        total = total - lax.dot_general(
            piece, tt, (((1,), (1,)), ((), ())), preferred_element_type=F32
        )
        total = total - lax.dot_general(
            tt, piece, (((0,), (0,)), ((), ())), preferred_element_type=F32
        )
    f_sum = occ[occ_at[0]] + occ[occ_at[1]]
    t = tt.astype(F32).T
    e_row = [virt[pl.ds(tiles[s], 1), :] for s in range(2)]
    e_col = [jnp.sum(jnp.where(row == col, e, 0.0), axis=1, keepdims=True) for e in e_row]
    keep = [mask[s].astype(F32) for s in range(2)]
    for a in range(2):
        for b in range(2):
            at = (slice(a * TILE, (a + 1) * TILE), slice(b * TILE, (b + 1) * TILE))
            delta = (e_col[a] + e_row[b]) - f_sum
            out[at] = (keep[a] * keep[b]) * (total[at] + delta * t[at])


def on_device(chips, amplitudes, integrals, pair_occ, dom_tiles, dom_mask, virt_energy, occ_energy):
    naux, wide = integrals.shape[2:]
    far = chips // 2
    vmem = pl.BlockSpec(memory_space=pltpu.VMEM)
    smem = pl.BlockSpec(memory_space=pltpu.SMEM)

    def call(kernel, n_in, shapes, name, small=0):
        return pl.pallas_call(
            kernel,
            in_specs=[smem] * small + [vmem] * n_in,
            out_specs=[vmem] * len(shapes),
            out_shape=[jax.ShapeDtypeStruct(*s) for s in shapes],
            compiler_params=pltpu.CompilerParams(vmem_limit_bytes=8 << 20),
            name=name,
        )

    def permute(x, hops, cross=False):
        pairs = []
        for chip in range(chips):
            for core in range(2):
                to = (chip + (1 - 2 * core) * hops) % chips
                pairs.append((chip * 2 + core, to * 2 + (core ^ int(cross))))
        return lax.ppermute(x, "aux", pairs)

    def pack(wanted, other):
        return call(
            functools.partial(pack_kernel, chips, wanted),
            2,
            [((2 * len(group), naux, wide), BF16) for group in wanted],
            "pack_rows",
        )(ints, other)

    def stop_sums(stop, owners, picks, scaled, other, received):
        return call(
            functools.partial(stop_kernel, chips, stop, owners, picks, scaled),
            2 + len(received),
            [((len(owners), ROWS, TILE), F32)],
            "stop_sums",
        )(ints, other, *received)[0]

    def pairs_at(d):
        return [(d, True)] if d == far else [(d, True), (d, False)]


    ints = integrals[:, 0]
    (other,) = call(
        functools.partial(split_kernel, chips), 1, [((chips, naux, wide), BF16)], "split_cores"
    )(ints)
    other = lax.ppermute(other, "aux", [(i, i ^ 1) for i in range(2 * chips)])

    to_first = list(range(far, FIRST, -1))
    to_second = list(range(FIRST - 1, SECOND, -1))
    to_owner = list(range(SECOND - 1, 0, -1))
    sends = pack([pairs_at(d) for d in to_first], other)
    first_rows = [permute(x, d - FIRST) for d, x in zip(to_first, sends)]
    owned = lax.all_to_all(amplitudes, "pair", split_axis=1, concat_axis=3, tiled=True)
    gate, owned, *first_rows = lax.optimization_barrier((other, owned, *first_rows))
    sends = pack([pairs_at(d) for d in to_second], gate)
    second_rows = [permute(x, d - SECOND) for d, x in zip(to_second, sends)]

    picks = [((0, None) if d == far else (0, 2), at) for at, d in enumerate(to_first)]
    x = stop_sums(FIRST, (True, False), picks, True, other, first_rows).astype(F16)
    moving = permute(x, FIRST - SECOND)

    gate = lax.optimization_barrier((other, x))[0]
    sends = pack([[(d, mine)] for d in to_owner for mine in (True, False)], gate)
    ways = [(d, n == 1) for d in to_owner for n in range(2)]
    owner_rows = [permute(x, *way) for way, x in zip(ways, sends)]
    picks = [((0, 2), at) for at in range(len(to_second))]
    local = stop_sums(SECOND, (True, False), picks, False, gate, second_rows)
    last = [add_on(moving[n : n + 1], local[n : n + 1])[0] for n in range(2)]
    *last, owner_rows = lax.optimization_barrier((*last, owner_rows))
    moving = [permute(last[n], SECOND, n == 1) for n in range(2)]

    gate = lax.optimization_barrier((other, last[1]))[0]
    picks = [((0,), at) for at in range(len(owner_rows))]
    local = stop_sums(0, (True,), picks, False, gate, owner_rows)
    sums = (decode(moving[0][None])[0] + decode(moving[1][None])[0] + local)[0]
    amps_t = jnp.swapaxes(owned[0, 0], 0, 1)

    (out,) = call(final_kernel, 3, [((2 * TILE, 2 * TILE), F32)], "residual", 4)(
        pair_occ.reshape(-1),
        dom_tiles.reshape(-1),
        dom_mask.reshape(-1),
        occ_energy,
        virt_energy.reshape(-1, TILE),
        sums,
        amps_t,
    )
    return out[None, None]


def solution(mesh):
    return jax.shard_map(
        functools.partial(on_device, mesh.shape["aux"] // 2),
        mesh=mesh,
        in_specs=(
            P("aux", None, None, "pair"),
            P(None, "pair", "aux", None),
            P("aux", "pair", None),
            P("aux", "pair", None),
            P("aux", "pair", None),
            P(),
            P(),
        ),
        out_specs=P("aux", "pair", None, None),
        check_vma=False,
    )
```

```python
import functools

import jax
import jax.numpy as jnp
from jax import lax
from jax.experimental import pallas as pl
from jax.experimental.pallas import tpu as pltpu
from jax.sharding import PartitionSpec as P

TILE = 128
FIRST, SECOND = 4, 2
H_ROWS, G_ROWS = 4 * TILE, 2 * TILE
DIAG = H_ROWS + G_ROWS
H_EXP, G_EXP = DIAG + 1, DIAG + 2
ROWS = DIAG + 16
F32 = jnp.float32
BF16 = jnp.bfloat16
F16 = jnp.float16


def here():
    me = lax.axis_index("aux")
    c = lax.rem(me, 2)
    return lax.div(me, 2), c, 1 - 2 * c


def toward(chips, distance):
    z, _, way = here()
    return lax.rem(z + way * distance + chips, chips)


def iotas():
    return (
        lax.broadcasted_iota(jnp.int32, (TILE, TILE), 0),
        lax.broadcasted_iota(jnp.int32, (TILE, TILE), 1),
    )


def exponent(*parts):
    top = None
    for part in parts:
        high = jnp.max(jnp.abs(part), axis=0, keepdims=True)
        top = high if top is None else jnp.maximum(top, high)
    top = jnp.max(top, axis=1, keepdims=True)
    power = 14.0 - jnp.floor(jnp.log2(jnp.maximum(top, 1e-30)))
    return jnp.broadcast_to(power, (1, TILE))


def packed_sum(blocks, out, scaled=False):
    total = None
    for block in blocks:
        term = lax.dot_general(
            block[:, : 2 * TILE], block, (((0,), (0,)), ((), ())), preferred_element_type=F32
        )
        total = term if total is None else total + term
    row, col = iotas()
    g00, g01 = total[:TILE, :TILE], total[:TILE, TILE : 2 * TILE]
    g11 = total[TILE:, TILE : 2 * TILE]
    h0, h1 = total[:, 2 * TILE : 3 * TILE], total[:, 3 * TILE :]
    fold = jnp.where(row <= col, g00, g11)
    diag = jnp.sum(jnp.where(row == col, g11, 0.0), axis=0, keepdims=True)
    e_h, e_g = exponent(h0, h1), exponent(g01, fold, diag)
    if scaled:
        by_h, by_g = jnp.exp2(e_h), jnp.exp2(e_g)
        h0, h1, g01, fold, diag = h0 * by_h, h1 * by_h, g01 * by_g, fold * by_g, diag * by_g
    out[: 2 * TILE] = h0
    out[2 * TILE : H_ROWS] = h1
    out[H_ROWS : H_ROWS + TILE] = g01
    out[H_ROWS + TILE : DIAG] = fold
    lines = lax.broadcasted_iota(jnp.int32, (ROWS - DIAG, TILE), 0)
    rest = jnp.where(lines == 0, diag, 0.0)
    rest = jnp.where(lines == H_EXP - DIAG, e_h, rest)
    out[DIAG:] = jnp.where(lines == G_EXP - DIAG, e_g, rest)


def scales(e_h, e_g):
    row = lax.broadcasted_iota(jnp.int32, (1, ROWS, TILE), 1)
    return row, jnp.where(row < H_ROWS, jnp.exp2(e_h), jnp.exp2(e_g))


def exponents(x):
    return x[:, H_EXP : H_EXP + 1], x[:, G_EXP : G_EXP + 1]


def decode(x):
    x = x.astype(F32)
    e_h, e_g = exponents(x)
    return x * scales(-e_h, -e_g)[1], e_h, e_g


def add_on(x, own):
    x, e_h, e_g = decode(x)
    own_h, own_g = exponents(own)
    e_h, e_g = jnp.minimum(e_h, own_h) - 1.0, jnp.minimum(e_g, own_g) - 1.0
    row, scale = scales(e_h, e_g)
    tail = jnp.where(row == H_EXP, e_h, e_g)
    return jnp.where(row <= DIAG, (x + own) * scale, tail).astype(F16)


def split_kernel(chips, ints, out):
    z, c, _ = here()
    near = chips // 2 - 1
    for d in range(1, near + 1):
        to = toward(chips, -d)
        out[2 * d - 2] = ints[2 * to + 1 - c]
        out[2 * d - 1] = ints[2 * to + c]
    out[2 * near] = ints[2 * lax.rem(z + near + 1, chips) + 1 - c]
    out[2 * near + 1] = ints[2 * z + 1 - c]


def chip_rows(chips, ints, other, distance, mine):
    c = here()[1]
    near = chips // 2 - 1
    if distance == 0:
        at = 2 * near + 1
    elif distance > near:
        at = 2 * near
    else:
        at = 2 * distance - 1 - int(mine)
    return [ints[2 * toward(chips, distance) + (c if mine else 1 - c)], other[at]]


def pack_kernel(chips, wanted, ints, other, *outs):
    for group, out in zip(wanted, outs):
        for n, row in enumerate(sum((chip_rows(chips, ints, other, *w) for w in group), [])):
            out[n] = row


def stop_kernel(chips, stop, owners, picks, scaled, ints, other, *rest):
    received, out = rest[:-1], rest[-1]
    for n, mine in enumerate(owners):
        blocks = chip_rows(chips, ints, other, stop, mine)
        for at, ref in picks:
            if at[n] is not None:
                blocks += [received[ref][at[n]], received[ref][at[n] + 1]]
        packed_sum(blocks, out.at[n], scaled)


def final_kernel(occ_at, tiles, mask, occ, virt, sums, amps_t, out):
    row, col = iotas()
    h = jnp.concatenate([sums[: 2 * TILE], sums[2 * TILE : H_ROWS]], axis=1)
    g01 = sums[H_ROWS : H_ROWS + TILE]
    fold = sums[H_ROWS + TILE : DIAG]
    diag = sums[DIAG : DIAG + 8][:1]
    above = jnp.where(row < col, fold, 0.0)
    below = jnp.where(row > col, fold, 0.0)
    g00 = jnp.where(row <= col, fold, 0.0) + above.T
    g11 = below + below.T + jnp.where(row == col, diag, 0.0)
    g = jnp.concatenate(
        [jnp.concatenate([g00, g01], axis=1), jnp.concatenate([g01.T, g11], axis=1)], axis=0
    )
    tt = amps_t[...]
    total = h
    rest = g
    for _ in range(3):
        piece = rest.astype(BF16)
        rest = rest - piece.astype(F32)
        total = total - lax.dot_general(
            piece, tt, (((1,), (1,)), ((), ())), preferred_element_type=F32
        )
        total = total - lax.dot_general(
            tt, piece, (((0,), (0,)), ((), ())), preferred_element_type=F32
        )
    f_sum = occ[occ_at[0]] + occ[occ_at[1]]
    t = tt.astype(F32).T
    e_row = [virt[pl.ds(tiles[s], 1), :] for s in range(2)]
    e_col = [jnp.sum(jnp.where(row == col, e, 0.0), axis=1, keepdims=True) for e in e_row]
    keep = [mask[s].astype(F32) for s in range(2)]
    for a in range(2):
        for b in range(2):
            at = (slice(a * TILE, (a + 1) * TILE), slice(b * TILE, (b + 1) * TILE))
            delta = (e_col[a] + e_row[b]) - f_sum
            out[at] = (keep[a] * keep[b]) * (total[at] + delta * t[at])


def on_device(chips, amplitudes, integrals, pair_occ, dom_tiles, dom_mask, virt_energy, occ_energy):
    naux, wide = integrals.shape[2:]
    far = chips // 2
    vmem = pl.BlockSpec(memory_space=pltpu.VMEM)
    smem = pl.BlockSpec(memory_space=pltpu.SMEM)

    def call(kernel, n_in, shapes, name, small=0):
        return pl.pallas_call(
            kernel,
            in_specs=[smem] * small + [vmem] * n_in,
            out_specs=[vmem] * len(shapes),
            out_shape=[jax.ShapeDtypeStruct(*s) for s in shapes],
            compiler_params=pltpu.CompilerParams(vmem_limit_bytes=8 << 20),
            name=name,
        )

    def permute(x, hops, cross=False):
        pairs = []
        for chip in range(chips):
            for core in range(2):
                to = (chip + (1 - 2 * core) * hops) % chips
                pairs.append((chip * 2 + core, to * 2 + (core ^ int(cross))))
        return lax.ppermute(x, "aux", pairs)

    def pack(wanted, other):
        return call(
            functools.partial(pack_kernel, chips, wanted),
            2,
            [((2 * len(group), naux, wide), BF16) for group in wanted],
            "pack_rows",
        )(ints, other)

    def stop_sums(stop, owners, picks, scaled, other, received):
        return call(
            functools.partial(stop_kernel, chips, stop, owners, picks, scaled),
            2 + len(received),
            [((len(owners), ROWS, TILE), F32)],
            "stop_sums",
        )(ints, other, *received)[0]

    def pairs_at(d):
        return [(d, True)] if d == far else [(d, True), (d, False)]


    ints = integrals[:, 0]
    (other,) = call(
        functools.partial(split_kernel, chips), 1, [((chips, naux, wide), BF16)], "split_cores"
    )(ints)
    other = lax.ppermute(other, "aux", [(i, i ^ 1) for i in range(2 * chips)])

    to_first = list(range(far, FIRST, -1))
    to_second = list(range(FIRST - 1, SECOND, -1))
    to_owner = list(range(SECOND - 1, 0, -1))
    sends = pack([pairs_at(d) for d in to_first], other)
    first_rows = [permute(x, d - FIRST) for d, x in zip(to_first, sends)]
    gate = lax.optimization_barrier((other, *sends))[0]
    sends = pack([pairs_at(d) for d in to_second], gate)
    second_rows = [permute(x, d - SECOND) for d, x in zip(to_second, sends)]
    amplitudes, first_rows[0] = lax.optimization_barrier((amplitudes, first_rows[0]))
    owned = lax.all_to_all(amplitudes, "pair", split_axis=1, concat_axis=3, tiled=True)

    picks = [((0, None) if d == far else (0, 2), at) for at, d in enumerate(to_first)]
    x = stop_sums(FIRST, (True, False), picks, True, other, first_rows).astype(F16)
    x, *second_rows = lax.optimization_barrier((x, *second_rows))
    moving = permute(x, FIRST - SECOND)

    gate = lax.optimization_barrier((other, x))[0]
    sends = pack([[(d, mine)] for d in to_owner for mine in (True, False)], gate)
    ways = [(d, n == 1) for d in to_owner for n in range(2)]
    owner_rows = [permute(x, *way) for way, x in zip(ways, sends)]
    picks = [((0, 2), at) for at in range(len(to_second))]
    gate, owned = lax.optimization_barrier((gate, owned))
    local = stop_sums(SECOND, (True, False), picks, False, gate, second_rows)
    last = [add_on(moving[n : n + 1], local[n : n + 1])[0] for n in range(2)]
    *last, owner_rows = lax.optimization_barrier((*last, owner_rows))
    moving = [permute(last[n], SECOND, n == 1) for n in range(2)]

    gate = lax.optimization_barrier((other, last[1]))[0]
    picks = [((0,), at) for at in range(len(owner_rows))]
    local = stop_sums(0, (True,), picks, False, gate, owner_rows)
    sums = (decode(moving[0][None])[0] + decode(moving[1][None])[0] + local)[0]
    amps_t = jnp.swapaxes(owned[0, 0], 0, 1)

    (out,) = call(final_kernel, 3, [((2 * TILE, 2 * TILE), F32)], "residual", 4)(
        pair_occ.reshape(-1),
        dom_tiles.reshape(-1),
        dom_mask.reshape(-1),
        occ_energy,
        virt_energy.reshape(-1, TILE),
        sums,
        amps_t,
    )
    return out[None, None]


def solution(mesh):
    return jax.shard_map(
        functools.partial(on_device, mesh.shape["aux"] // 2),
        mesh=mesh,
        in_specs=(
            P("aux", None, None, "pair"),
            P(None, "pair", "aux", None),
            P("aux", "pair", None),
            P("aux", "pair", None),
            P("aux", "pair", None),
            P(),
            P(),
        ),
        out_specs=P("aux", "pair", None, None),
        check_vma=False,
    )
```

```python
import functools

import jax
import jax.numpy as jnp
from jax import lax
from jax.experimental import pallas as pl
from jax.experimental.pallas import tpu as pltpu
from jax.sharding import PartitionSpec as P

TILE = 128
FIRST, SECOND = 4, 2
H_ROWS, G_ROWS = 4 * TILE, 2 * TILE
DIAG = H_ROWS + G_ROWS
H_EXP, G_EXP = DIAG + 1, DIAG + 2
ROWS = DIAG + 16
F32 = jnp.float32
BF16 = jnp.bfloat16
F16 = jnp.float16


def here():
    me = lax.axis_index("aux")
    c = lax.rem(me, 2)
    return lax.div(me, 2), c, 1 - 2 * c


def toward(chips, distance):
    z, _, way = here()
    return lax.rem(z + way * distance + chips, chips)


def iotas():
    return (
        lax.broadcasted_iota(jnp.int32, (TILE, TILE), 0),
        lax.broadcasted_iota(jnp.int32, (TILE, TILE), 1),
    )


def exponent(*parts):
    top = None
    for part in parts:
        high = jnp.max(jnp.abs(part), axis=0, keepdims=True)
        top = high if top is None else jnp.maximum(top, high)
    top = jnp.max(top, axis=1, keepdims=True)
    power = 14.0 - jnp.floor(jnp.log2(jnp.maximum(top, 1e-30)))
    return jnp.broadcast_to(power, (1, TILE))


def packed_sum(blocks, out, scaled=False):
    total = None
    for block in blocks:
        term = lax.dot_general(
            block[:, : 2 * TILE], block, (((0,), (0,)), ((), ())), preferred_element_type=F32
        )
        total = term if total is None else total + term
    row, col = iotas()
    g00, g01 = total[:TILE, :TILE], total[:TILE, TILE : 2 * TILE]
    g11 = total[TILE:, TILE : 2 * TILE]
    h0, h1 = total[:, 2 * TILE : 3 * TILE], total[:, 3 * TILE :]
    fold = jnp.where(row <= col, g00, g11)
    diag = jnp.sum(jnp.where(row == col, g11, 0.0), axis=0, keepdims=True)
    e_h, e_g = exponent(h0, h1), exponent(g01, fold, diag)
    if scaled:
        by_h, by_g = jnp.exp2(e_h), jnp.exp2(e_g)
        h0, h1, g01, fold, diag = h0 * by_h, h1 * by_h, g01 * by_g, fold * by_g, diag * by_g
    out[: 2 * TILE] = h0
    out[2 * TILE : H_ROWS] = h1
    out[H_ROWS : H_ROWS + TILE] = g01
    out[H_ROWS + TILE : DIAG] = fold
    lines = lax.broadcasted_iota(jnp.int32, (ROWS - DIAG, TILE), 0)
    rest = jnp.where(lines == 0, diag, 0.0)
    rest = jnp.where(lines == H_EXP - DIAG, e_h, rest)
    out[DIAG:] = jnp.where(lines == G_EXP - DIAG, e_g, rest)


def scales(e_h, e_g):
    row = lax.broadcasted_iota(jnp.int32, (1, ROWS, TILE), 1)
    return row, jnp.where(row < H_ROWS, jnp.exp2(e_h), jnp.exp2(e_g))


def exponents(x):
    return x[:, H_EXP : H_EXP + 1], x[:, G_EXP : G_EXP + 1]


def decode(x):
    x = x.astype(F32)
    e_h, e_g = exponents(x)
    return x * scales(-e_h, -e_g)[1], e_h, e_g


def add_on(x, own):
    x, e_h, e_g = decode(x)
    own_h, own_g = exponents(own)
    e_h, e_g = jnp.minimum(e_h, own_h) - 1.0, jnp.minimum(e_g, own_g) - 1.0
    row, scale = scales(e_h, e_g)
    tail = jnp.where(row == H_EXP, e_h, e_g)
    return jnp.where(row <= DIAG, (x + own) * scale, tail).astype(F16)


def split_kernel(chips, ints, out):
    z, c, _ = here()
    near = chips // 2 - 1
    for d in range(1, near + 1):
        to = toward(chips, -d)
        out[2 * d - 2] = ints[2 * to + 1 - c]
        out[2 * d - 1] = ints[2 * to + c]
    out[2 * near] = ints[2 * lax.rem(z + near + 1, chips) + 1 - c]
    out[2 * near + 1] = ints[2 * z + 1 - c]


def chip_rows(chips, ints, other, distance, mine):
    c = here()[1]
    near = chips // 2 - 1
    if distance == 0:
        at = 2 * near + 1
    elif distance > near:
        at = 2 * near
    else:
        at = 2 * distance - 1 - int(mine)
    return [ints[2 * toward(chips, distance) + (c if mine else 1 - c)], other[at]]


def pack_kernel(chips, wanted, ints, other, *rest):
    arrived, outs = rest[: -len(wanted)], rest[-len(wanted) :]
    for group, out in zip(wanted, outs):
        if not group:
            out[...] = arrived[0][-2:]
        for n, row in enumerate(sum((chip_rows(chips, ints, other, *w) for w in group), [])):
            out[n] = row


def stop_kernel(chips, stop, owners, picks, scaled, ints, other, *rest):
    received, out = rest[:-1], rest[-1]
    for n, mine in enumerate(owners):
        blocks = chip_rows(chips, ints, other, stop, mine)
        for at, ref in picks:
            if at[n] is not None:
                blocks += [received[ref][at[n]], received[ref][at[n] + 1]]
        packed_sum(blocks, out.at[n], scaled)


def final_kernel(occ_at, tiles, mask, occ, virt, sums, amps_t, out):
    row, col = iotas()
    h = jnp.concatenate([sums[: 2 * TILE], sums[2 * TILE : H_ROWS]], axis=1)
    g01 = sums[H_ROWS : H_ROWS + TILE]
    fold = sums[H_ROWS + TILE : DIAG]
    diag = sums[DIAG : DIAG + 8][:1]
    above = jnp.where(row < col, fold, 0.0)
    below = jnp.where(row > col, fold, 0.0)
    g00 = jnp.where(row <= col, fold, 0.0) + above.T
    g11 = below + below.T + jnp.where(row == col, diag, 0.0)
    g = jnp.concatenate(
        [jnp.concatenate([g00, g01], axis=1), jnp.concatenate([g01.T, g11], axis=1)], axis=0
    )
    tt = amps_t[...]
    total = h
    rest = g
    for _ in range(3):
        piece = rest.astype(BF16)
        rest = rest - piece.astype(F32)
        total = total - lax.dot_general(
            piece, tt, (((1,), (1,)), ((), ())), preferred_element_type=F32
        )
        total = total - lax.dot_general(
            tt, piece, (((0,), (0,)), ((), ())), preferred_element_type=F32
        )
    f_sum = occ[occ_at[0]] + occ[occ_at[1]]
    t = tt.astype(F32).T
    e_row = [virt[pl.ds(tiles[s], 1), :] for s in range(2)]
    e_col = [jnp.sum(jnp.where(row == col, e, 0.0), axis=1, keepdims=True) for e in e_row]
    keep = [mask[s].astype(F32) for s in range(2)]
    for a in range(2):
        for b in range(2):
            at = (slice(a * TILE, (a + 1) * TILE), slice(b * TILE, (b + 1) * TILE))
            delta = (e_col[a] + e_row[b]) - f_sum
            out[at] = (keep[a] * keep[b]) * (total[at] + delta * t[at])


def on_device(chips, amplitudes, integrals, pair_occ, dom_tiles, dom_mask, virt_energy, occ_energy):
    naux, wide = integrals.shape[2:]
    far = chips // 2
    vmem = pl.BlockSpec(memory_space=pltpu.VMEM)
    smem = pl.BlockSpec(memory_space=pltpu.SMEM)

    def call(kernel, n_in, shapes, name, small=0):
        return pl.pallas_call(
            kernel,
            in_specs=[smem] * small + [vmem] * n_in,
            out_specs=[vmem] * len(shapes),
            out_shape=[jax.ShapeDtypeStruct(*s) for s in shapes],
            compiler_params=pltpu.CompilerParams(vmem_limit_bytes=8 << 20),
            name=name,
        )

    def permute(x, hops, cross=False):
        pairs = []
        for chip in range(chips):
            for core in range(2):
                to = (chip + (1 - 2 * core) * hops) % chips
                pairs.append((chip * 2 + core, to * 2 + (core ^ int(cross))))
        return lax.ppermute(x, "aux", pairs)

    def pack(wanted, other, *arrived):
        return call(
            functools.partial(pack_kernel, chips, wanted),
            2 + len(arrived),
            [((2 * (len(group) or 1), naux, wide), BF16) for group in wanted],
            "pack_rows",
        )(ints, other, *arrived)

    def stop_sums(stop, owners, picks, scaled, other, received):
        return call(
            functools.partial(stop_kernel, chips, stop, owners, picks, scaled),
            2 + len(received),
            [((len(owners), ROWS, TILE), F32)],
            "stop_sums",
        )(ints, other, *received)[0]


    owned = lax.all_to_all(amplitudes, "pair", split_axis=1, concat_axis=3, tiled=True)
    to_second = list(range(FIRST - 1, SECOND, -1))
    to_owner = list(range(SECOND - 1, 0, -1))

    ints = integrals[:, 0]
    (other,) = call(
        functools.partial(split_kernel, chips), 1, [((chips, naux, wide), BF16)], "split_cores"
    )(ints)
    other = lax.ppermute(other, "aux", [(i, i ^ 1) for i in range(2 * chips)])

    (send,) = pack([[(far - 1, True), (far - 1, False), (far, True)]], other)
    arrived = permute(send, 1)
    gate, owned = lax.optimization_barrier((other, owned, send))[:2]
    sends = pack([[(d, True), (d, False)] for d in to_second], gate)
    second_rows = [permute(x, d - SECOND) for d, x in zip(to_second, sends)]
    (onward,) = pack([[]], other, arrived)
    first_rows = [arrived, permute(onward, 1)]

    picks = [((0, 2), 0), ((0, None), 1)]
    x = stop_sums(FIRST, (True, False), picks, True, other, first_rows).astype(F16)
    moving = permute(x, FIRST - SECOND)

    gate = lax.optimization_barrier((other, x))[0]
    sends = pack([[(d, mine)] for d in to_owner for mine in (True, False)], gate)
    ways = [(d, n == 1) for d in to_owner for n in range(2)]
    owner_rows = [permute(x, *way) for way, x in zip(ways, sends)]
    picks = [((0, 2), at) for at in range(len(to_second))]
    local = stop_sums(SECOND, (True, False), picks, False, gate, second_rows)
    last = [add_on(moving[n : n + 1], local[n : n + 1])[0] for n in range(2)]
    *last, owner_rows = lax.optimization_barrier((*last, owner_rows))
    moving = [permute(last[n], SECOND, n == 1) for n in range(2)]

    gate = lax.optimization_barrier((other, last[1]))[0]
    picks = [((0,), at) for at in range(len(owner_rows))]
    local = stop_sums(0, (True,), picks, False, gate, owner_rows)
    sums = (decode(moving[0][None])[0] + decode(moving[1][None])[0] + local)[0]
    amps_t = jnp.swapaxes(owned[0, 0], 0, 1)

    (out,) = call(final_kernel, 3, [((2 * TILE, 2 * TILE), F32)], "residual", 4)(
        pair_occ.reshape(-1),
        dom_tiles.reshape(-1),
        dom_mask.reshape(-1),
        occ_energy,
        virt_energy.reshape(-1, TILE),
        sums,
        amps_t,
    )
    return out[None, None]


def solution(mesh):
    return jax.shard_map(
        functools.partial(on_device, mesh.shape["aux"] // 2),
        mesh=mesh,
        in_specs=(
            P("aux", None, None, "pair"),
            P(None, "pair", "aux", None),
            P("aux", "pair", None),
            P("aux", "pair", None),
            P("aux", "pair", None),
            P(),
            P(),
        ),
        out_specs=P("aux", "pair", None, None),
        check_vma=False,
    )
```

```python
import functools

import jax
import jax.numpy as jnp
from jax import lax
from jax.experimental import pallas as pl
from jax.experimental.pallas import tpu as pltpu
from jax.sharding import PartitionSpec as P

TILE = 128
STOP = 2
H_ROWS, G_ROWS = 4 * TILE, 2 * TILE
DIAG = H_ROWS + G_ROWS
H_EXP, G_EXP = DIAG + 1, DIAG + 2
ROWS = DIAG + 16
F32 = jnp.float32
BF16 = jnp.bfloat16
F16 = jnp.float16


def here():
    me = lax.axis_index("aux")
    c = lax.rem(me, 2)
    return lax.div(me, 2), c, 1 - 2 * c


def toward(chips, distance):
    z, _, way = here()
    return lax.rem(z + way * distance + chips, chips)


def iotas():
    return (
        lax.broadcasted_iota(jnp.int32, (TILE, TILE), 0),
        lax.broadcasted_iota(jnp.int32, (TILE, TILE), 1),
    )


def exponent(*parts):
    top = None
    for part in parts:
        high = jnp.max(jnp.abs(part), axis=0, keepdims=True)
        top = high if top is None else jnp.maximum(top, high)
    top = jnp.max(top, axis=1, keepdims=True)
    power = 14.0 - jnp.floor(jnp.log2(jnp.maximum(top, 1e-30)))
    return jnp.broadcast_to(power, (1, TILE))


def packed_sum(blocks, out, scaled=False):
    total = None
    for block in blocks:
        term = lax.dot_general(
            block[:, : 2 * TILE], block, (((0,), (0,)), ((), ())), preferred_element_type=F32
        )
        total = term if total is None else total + term
    row, col = iotas()
    g00, g01 = total[:TILE, :TILE], total[:TILE, TILE : 2 * TILE]
    g11 = total[TILE:, TILE : 2 * TILE]
    h0, h1 = total[:, 2 * TILE : 3 * TILE], total[:, 3 * TILE :]
    fold = jnp.where(row <= col, g00, g11)
    diag = jnp.sum(jnp.where(row == col, g11, 0.0), axis=0, keepdims=True)
    e_h, e_g = exponent(h0, h1), exponent(g01, fold, diag)
    if scaled:
        by_h, by_g = jnp.exp2(e_h), jnp.exp2(e_g)
        h0, h1, g01, fold, diag = h0 * by_h, h1 * by_h, g01 * by_g, fold * by_g, diag * by_g
    out[: 2 * TILE] = h0
    out[2 * TILE : H_ROWS] = h1
    out[H_ROWS : H_ROWS + TILE] = g01
    out[H_ROWS + TILE : DIAG] = fold
    lines = lax.broadcasted_iota(jnp.int32, (ROWS - DIAG, TILE), 0)
    rest = jnp.where(lines == 0, diag, 0.0)
    rest = jnp.where(lines == H_EXP - DIAG, e_h, rest)
    out[DIAG:] = jnp.where(lines == G_EXP - DIAG, e_g, rest)


def scales(e_h, e_g):
    row = lax.broadcasted_iota(jnp.int32, (1, ROWS, TILE), 1)
    return row, jnp.where(row < H_ROWS, jnp.exp2(e_h), jnp.exp2(e_g))


def exponents(x):
    return x[:, H_EXP : H_EXP + 1], x[:, G_EXP : G_EXP + 1]


def decode(x):
    x = x.astype(F32)
    e_h, e_g = exponents(x)
    return x * scales(-e_h, -e_g)[1], e_h, e_g


def split_kernel(chips, ints, out):
    z, c, _ = here()
    near = chips // 2 - 1
    for d in range(1, near + 1):
        to = toward(chips, -d)
        out[2 * d - 2] = ints[2 * to + 1 - c]
        out[2 * d - 1] = ints[2 * to + c]
    out[2 * near] = ints[2 * lax.rem(z + near + 1, chips) + 1 - c]
    out[2 * near + 1] = ints[2 * z + 1 - c]


def chip_rows(chips, ints, other, distance, mine):
    c = here()[1]
    near = chips // 2 - 1
    if distance == 0:
        at = 2 * near + 1
    elif distance > near:
        at = 2 * near
    else:
        at = 2 * distance - 1 - int(mine)
    return [ints[2 * toward(chips, distance) + (c if mine else 1 - c)], other[at]]


def pack_kernel(chips, wanted, ints, other, *outs):
    for group, out in zip(wanted, outs):
        for n, row in enumerate(sum((chip_rows(chips, ints, other, *w) for w in group), [])):
            out[n] = row


def stop_kernel(chips, stop, owners, picks, scaled, ints, other, *rest):
    received, out = rest[:-1], rest[-1]
    for n, mine in enumerate(owners):
        blocks = chip_rows(chips, ints, other, stop, mine)
        for at, ref in picks:
            if at[n] is not None:
                blocks += [received[ref][at[n]], received[ref][at[n] + 1]]
        packed_sum(blocks, out.at[n], scaled)


def final_kernel(occ_at, tiles, mask, occ, virt, sums, amps_t, out):
    row, col = iotas()
    h = jnp.concatenate([sums[: 2 * TILE], sums[2 * TILE : H_ROWS]], axis=1)
    g01 = sums[H_ROWS : H_ROWS + TILE]
    fold = sums[H_ROWS + TILE : DIAG]
    diag = sums[DIAG : DIAG + 8][:1]
    above = jnp.where(row < col, fold, 0.0)
    below = jnp.where(row > col, fold, 0.0)
    g00 = jnp.where(row <= col, fold, 0.0) + above.T
    g11 = below + below.T + jnp.where(row == col, diag, 0.0)
    g = jnp.concatenate(
        [jnp.concatenate([g00, g01], axis=1), jnp.concatenate([g01.T, g11], axis=1)], axis=0
    )
    tt = amps_t[...]
    total = h
    rest = g
    for _ in range(3):
        piece = rest.astype(BF16)
        rest = rest - piece.astype(F32)
        total = total - lax.dot_general(
            piece, tt, (((1,), (1,)), ((), ())), preferred_element_type=F32
        )
        total = total - lax.dot_general(
            tt, piece, (((0,), (0,)), ((), ())), preferred_element_type=F32
        )
    f_sum = occ[occ_at[0]] + occ[occ_at[1]]
    t = tt.astype(F32).T
    e_row = [virt[pl.ds(tiles[s], 1), :] for s in range(2)]
    e_col = [jnp.sum(jnp.where(row == col, e, 0.0), axis=1, keepdims=True) for e in e_row]
    keep = [mask[s].astype(F32) for s in range(2)]
    for a in range(2):
        for b in range(2):
            at = (slice(a * TILE, (a + 1) * TILE), slice(b * TILE, (b + 1) * TILE))
            delta = (e_col[a] + e_row[b]) - f_sum
            out[at] = (keep[a] * keep[b]) * (total[at] + delta * t[at])


def on_device(chips, amplitudes, integrals, pair_occ, dom_tiles, dom_mask, virt_energy, occ_energy):
    naux, wide = integrals.shape[2:]
    far = chips // 2
    vmem = pl.BlockSpec(memory_space=pltpu.VMEM)
    smem = pl.BlockSpec(memory_space=pltpu.SMEM)

    def call(kernel, n_in, shapes, name, small=0):
        return pl.pallas_call(
            kernel,
            in_specs=[smem] * small + [vmem] * n_in,
            out_specs=[vmem] * len(shapes),
            out_shape=[jax.ShapeDtypeStruct(*s) for s in shapes],
            compiler_params=pltpu.CompilerParams(vmem_limit_bytes=8 << 20),
            name=name,
        )

    def permute(x, hops, cross=False):
        pairs = []
        for chip in range(chips):
            for core in range(2):
                to = (chip + (1 - 2 * core) * hops) % chips
                pairs.append((chip * 2 + core, to * 2 + (core ^ int(cross))))
        return lax.ppermute(x, "aux", pairs)

    def pack(wanted, other):
        return call(
            functools.partial(pack_kernel, chips, wanted),
            2,
            [((2 * len(group), naux, wide), BF16) for group in wanted],
            "pack_rows",
        )(ints, other)

    def stop_sums(stop, owners, picks, scaled, other, received):
        return call(
            functools.partial(stop_kernel, chips, stop, owners, picks, scaled),
            2 + len(received),
            [((len(owners), ROWS, TILE), F32)],
            "stop_sums",
        )(ints, other, *received)[0]

    def pairs_at(d):
        return [(d, True)] if d == far else [(d, True), (d, False)]


    ints = integrals[:, 0]
    (other,) = call(
        functools.partial(split_kernel, chips), 1, [((chips, naux, wide), BF16)], "split_cores"
    )(ints)
    other = lax.ppermute(other, "aux", [(i, i ^ 1) for i in range(2 * chips)])

    to_stop = list(range(far, STOP, -1))
    sends = pack([pairs_at(d) for d in to_stop], other)
    rows = [permute(x, d - STOP) for d, x in zip(to_stop, sends)]
    owned = lax.all_to_all(amplitudes, "pair", split_axis=1, concat_axis=3, tiled=True)

    picks = [((0, None) if d == far else (0, 2), at) for at, d in enumerate(to_stop)]
    moving = []
    for n, mine in enumerate((True, False)):
        x = stop_sums(STOP, (mine,), [((at[n],), ref) for at, ref in picks], True, other, rows)
        x = x[0].astype(F16)
        if n == 0:
            x, owned = lax.optimization_barrier((x, owned))
        moving.append(permute(x, STOP, n == 1))

    gate = lax.optimization_barrier((other, x))[0]
    to_owner = [(d, n) for d in range(STOP - 1, 0, -1) for n in range(2)]
    sends = pack([[(d, n == 0)] for d, n in to_owner], gate)
    rows = [permute(x, d, n == 1) for (d, n), x in zip(to_owner, sends)]
    picks = [((0,), at) for at in range(len(rows))]
    local = stop_sums(0, (True,), picks, False, gate, rows)
    sums = (decode(moving[0][None])[0] + decode(moving[1][None])[0] + local)[0]
    amps_t = jnp.swapaxes(owned[0, 0], 0, 1)

    (out,) = call(final_kernel, 3, [((2 * TILE, 2 * TILE), F32)], "residual", 4)(
        pair_occ.reshape(-1),
        dom_tiles.reshape(-1),
        dom_mask.reshape(-1),
        occ_energy,
        virt_energy.reshape(-1, TILE),
        sums,
        amps_t,
    )
    return out[None, None]


def solution(mesh):
    return jax.shard_map(
        functools.partial(on_device, mesh.shape["aux"] // 2),
        mesh=mesh,
        in_specs=(
            P("aux", None, None, "pair"),
            P(None, "pair", "aux", None),
            P("aux", "pair", None),
            P("aux", "pair", None),
            P("aux", "pair", None),
            P(),
            P(),
        ),
        out_specs=P("aux", "pair", None, None),
        check_vma=False,
    )
```

```python
import functools

import jax
import jax.numpy as jnp
from jax import lax
from jax.experimental import pallas as pl
from jax.experimental.pallas import tpu as pltpu
from jax.sharding import PartitionSpec as P

TILE = 128
STOP = 2
H_ROWS, G_ROWS = 4 * TILE, 2 * TILE
DIAG = H_ROWS + G_ROWS
H_EXP, G_EXP = DIAG + 1, DIAG + 2
ROWS = DIAG + 16
F32 = jnp.float32
BF16 = jnp.bfloat16
F16 = jnp.float16


def here():
    me = lax.axis_index("aux")
    c = lax.rem(me, 2)
    return lax.div(me, 2), c, 1 - 2 * c


def toward(chips, distance):
    z, _, way = here()
    return lax.rem(z + way * distance + chips, chips)


def iotas():
    return (
        lax.broadcasted_iota(jnp.int32, (TILE, TILE), 0),
        lax.broadcasted_iota(jnp.int32, (TILE, TILE), 1),
    )


def exponent(*parts):
    top = None
    for part in parts:
        high = jnp.max(jnp.abs(part), axis=0, keepdims=True)
        top = high if top is None else jnp.maximum(top, high)
    top = jnp.max(top, axis=1, keepdims=True)
    power = 14.0 - jnp.floor(jnp.log2(jnp.maximum(top, 1e-30)))
    return jnp.broadcast_to(power, (1, TILE))


def packed_sum(blocks, out, scaled=False):
    total = None
    for block in blocks:
        term = lax.dot_general(
            block[:, : 2 * TILE], block, (((0,), (0,)), ((), ())), preferred_element_type=F32
        )
        total = term if total is None else total + term
    row, col = iotas()
    g00, g01 = total[:TILE, :TILE], total[:TILE, TILE : 2 * TILE]
    g11 = total[TILE:, TILE : 2 * TILE]
    h0, h1 = total[:, 2 * TILE : 3 * TILE], total[:, 3 * TILE :]
    fold = jnp.where(row <= col, g00, g11)
    diag = jnp.sum(jnp.where(row == col, g11, 0.0), axis=0, keepdims=True)
    e_h, e_g = exponent(h0, h1), exponent(g01, fold, diag)
    if scaled:
        by_h, by_g = jnp.exp2(e_h), jnp.exp2(e_g)
        h0, h1, g01, fold, diag = h0 * by_h, h1 * by_h, g01 * by_g, fold * by_g, diag * by_g
    out[: 2 * TILE] = h0
    out[2 * TILE : H_ROWS] = h1
    out[H_ROWS : H_ROWS + TILE] = g01
    out[H_ROWS + TILE : DIAG] = fold
    lines = lax.broadcasted_iota(jnp.int32, (ROWS - DIAG, TILE), 0)
    rest = jnp.where(lines == 0, diag, 0.0)
    rest = jnp.where(lines == H_EXP - DIAG, e_h, rest)
    out[DIAG:] = jnp.where(lines == G_EXP - DIAG, e_g, rest)


def scales(e_h, e_g):
    row = lax.broadcasted_iota(jnp.int32, (1, ROWS, TILE), 1)
    return row, jnp.where(row < H_ROWS, jnp.exp2(e_h), jnp.exp2(e_g))


def exponents(x):
    return x[:, H_EXP : H_EXP + 1], x[:, G_EXP : G_EXP + 1]


def decode(x):
    x = x.astype(F32)
    e_h, e_g = exponents(x)
    return x * scales(-e_h, -e_g)[1], e_h, e_g


def split_kernel(chips, ints, out):
    z, c, _ = here()
    near = chips // 2 - 1
    for d in range(1, near + 1):
        to = toward(chips, -d)
        out[2 * d - 2] = ints[2 * to + 1 - c]
        out[2 * d - 1] = ints[2 * to + c]
    out[2 * near] = ints[2 * lax.rem(z + near + 1, chips) + 1 - c]
    out[2 * near + 1] = ints[2 * z + 1 - c]


def chip_rows(chips, ints, other, distance, mine):
    c = here()[1]
    near = chips // 2 - 1
    if distance == 0:
        at = 2 * near + 1
    elif distance > near:
        at = 2 * near
    else:
        at = 2 * distance - 1 - int(mine)
    return [ints[2 * toward(chips, distance) + (c if mine else 1 - c)], other[at]]


def pack_kernel(chips, wanted, ints, other, *outs):
    for group, out in zip(wanted, outs):
        for n, row in enumerate(sum((chip_rows(chips, ints, other, *w) for w in group), [])):
            out[n] = row


def stop_kernel(chips, stop, owners, picks, scaled, ints, other, *rest):
    received, outs = rest[: -len(owners)], rest[-len(owners) :]
    for n, mine in enumerate(owners):
        blocks = chip_rows(chips, ints, other, stop, mine)
        for at, ref in picks:
            if at[n] is not None:
                blocks += [received[ref][at[n]], received[ref][at[n] + 1]]
        packed_sum(blocks, outs[n], scaled)


def final_kernel(occ_at, tiles, mask, occ, virt, sums, amps_t, out):
    row, col = iotas()
    h = jnp.concatenate([sums[: 2 * TILE], sums[2 * TILE : H_ROWS]], axis=1)
    g01 = sums[H_ROWS : H_ROWS + TILE]
    fold = sums[H_ROWS + TILE : DIAG]
    diag = sums[DIAG : DIAG + 8][:1]
    above = jnp.where(row < col, fold, 0.0)
    below = jnp.where(row > col, fold, 0.0)
    g00 = jnp.where(row <= col, fold, 0.0) + above.T
    g11 = below + below.T + jnp.where(row == col, diag, 0.0)
    g = jnp.concatenate(
        [jnp.concatenate([g00, g01], axis=1), jnp.concatenate([g01.T, g11], axis=1)], axis=0
    )
    tt = amps_t[...]
    total = h
    rest = g
    for _ in range(2):
        piece = rest.astype(BF16)
        rest = rest - piece.astype(F32)
        total = total - lax.dot_general(
            piece, tt, (((1,), (1,)), ((), ())), preferred_element_type=F32
        )
        total = total - lax.dot_general(
            tt, piece, (((0,), (0,)), ((), ())), preferred_element_type=F32
        )
    f_sum = occ[occ_at[0]] + occ[occ_at[1]]
    t = tt.astype(F32).T
    e_row = [virt[pl.ds(tiles[s], 1), :] for s in range(2)]
    e_col = [jnp.sum(jnp.where(row == col, e, 0.0), axis=1, keepdims=True) for e in e_row]
    keep = [mask[s].astype(F32) for s in range(2)]
    for a in range(2):
        for b in range(2):
            at = (slice(a * TILE, (a + 1) * TILE), slice(b * TILE, (b + 1) * TILE))
            delta = (e_col[a] + e_row[b]) - f_sum
            out[at] = (keep[a] * keep[b]) * (total[at] + delta * t[at])


def on_device(chips, amplitudes, integrals, pair_occ, dom_tiles, dom_mask, virt_energy, occ_energy):
    naux, wide = integrals.shape[2:]
    far = chips // 2
    vmem = pl.BlockSpec(memory_space=pltpu.VMEM)
    smem = pl.BlockSpec(memory_space=pltpu.SMEM)

    def call(kernel, n_in, shapes, name, small=0):
        return pl.pallas_call(
            kernel,
            in_specs=[smem] * small + [vmem] * n_in,
            out_specs=[vmem] * len(shapes),
            out_shape=[jax.ShapeDtypeStruct(*s) for s in shapes],
            compiler_params=pltpu.CompilerParams(vmem_limit_bytes=8 << 20),
            name=name,
        )

    def permute(x, hops, cross=False):
        pairs = []
        for chip in range(chips):
            for core in range(2):
                to = (chip + (1 - 2 * core) * hops) % chips
                pairs.append((chip * 2 + core, to * 2 + (core ^ int(cross))))
        return lax.ppermute(x, "aux", pairs)

    def pack(wanted, other):
        return call(
            functools.partial(pack_kernel, chips, wanted),
            2,
            [((2 * len(group), naux, wide), BF16) for group in wanted],
            "pack_rows",
        )(ints, other)

    def stop_sums(stop, owners, picks, scaled, other, received):
        return call(
            functools.partial(stop_kernel, chips, stop, owners, picks, scaled),
            2 + len(received),
            [((ROWS, TILE), F32)] * len(owners),
            "stop_sums",
        )(ints, other, *received)

    def pairs_at(d):
        return [(d, True)] if d == far else [(d, True), (d, False)]


    ints = integrals[:, 0]
    (other,) = call(
        functools.partial(split_kernel, chips), 1, [((chips, naux, wide), BF16)], "split_cores"
    )(ints)
    other = lax.ppermute(other, "aux", [(i, i ^ 1) for i in range(2 * chips)])

    to_stop = list(range(far, STOP, -1))
    sends = pack([pairs_at(d) for d in to_stop], other)
    rows = [permute(x, d - STOP) for d, x in zip(to_stop, sends)]
    owned = lax.all_to_all(amplitudes, "pair", split_axis=1, concat_axis=3, tiled=True)

    picks = [((0, None) if d == far else (0, 2), at) for at, d in enumerate(to_stop)]
    both = stop_sums(STOP, (True, False), picks, True, other, rows)
    both, owned = lax.optimization_barrier((both, owned))
    moving = []
    for n in range(2):
        x = both[n].astype(F16)
        moving.append(permute(x, STOP, n == 1))

    gate = lax.optimization_barrier((other, x))[0]
    to_owner = [(d, n) for d in range(STOP - 1, 0, -1) for n in range(2)]
    sends = pack([[(d, n == 0)] for d, n in to_owner], gate)
    rows = [permute(x, d, n == 1) for (d, n), x in zip(to_owner, sends)]
    picks = [((0,), at) for at in range(len(rows))]
    gate, *moving = lax.optimization_barrier((gate, *moving))
    local = stop_sums(0, (True,), picks, False, gate, rows)
    sums = decode(moving[0][None])[0][0] + decode(moving[1][None])[0][0] + local[0]
    amps_t = jnp.swapaxes(owned[0, 0], 0, 1)

    (out,) = call(final_kernel, 3, [((2 * TILE, 2 * TILE), F32)], "residual", 4)(
        pair_occ.reshape(-1),
        dom_tiles.reshape(-1),
        dom_mask.reshape(-1),
        occ_energy,
        virt_energy.reshape(-1, TILE),
        sums,
        amps_t,
    )
    return out[None, None]


def solution(mesh):
    return jax.shard_map(
        functools.partial(on_device, mesh.shape["aux"] // 2),
        mesh=mesh,
        in_specs=(
            P("aux", None, None, "pair"),
            P(None, "pair", "aux", None),
            P("aux", "pair", None),
            P("aux", "pair", None),
            P("aux", "pair", None),
            P(),
            P(),
        ),
        out_specs=P("aux", "pair", None, None),
        check_vma=False,
    )
```

```python
import functools

import jax
import jax.numpy as jnp
from jax import lax
from jax.experimental import pallas as pl
from jax.experimental.pallas import tpu as pltpu
from jax.sharding import PartitionSpec as P

TILE = 128
FIRST, SECOND = 4, 2
H_ROWS, G_ROWS = 4 * TILE, 2 * TILE
DIAG = H_ROWS + G_ROWS
H_EXP, G_EXP = DIAG + 1, DIAG + 2
ROWS = DIAG + 16
F32 = jnp.float32
BF16 = jnp.bfloat16
F16 = jnp.float16


def here():
    me = lax.axis_index("aux")
    c = lax.rem(me, 2)
    return lax.div(me, 2), c, 1 - 2 * c


def toward(chips, distance):
    z, _, way = here()
    return lax.rem(z + way * distance + chips, chips)


def iotas():
    return (
        lax.broadcasted_iota(jnp.int32, (TILE, TILE), 0),
        lax.broadcasted_iota(jnp.int32, (TILE, TILE), 1),
    )


def exponent(*parts):
    top = None
    for part in parts:
        high = jnp.max(jnp.abs(part), axis=0, keepdims=True)
        top = high if top is None else jnp.maximum(top, high)
    top = jnp.max(top, axis=1, keepdims=True)
    power = 14.0 - jnp.floor(jnp.log2(jnp.maximum(top, 1e-30)))
    return jnp.broadcast_to(power, (1, TILE))


def packed_sum(blocks, out, scaled=False):
    total = None
    for block in blocks:
        term = lax.dot_general(
            block[:, : 2 * TILE], block, (((0,), (0,)), ((), ())), preferred_element_type=F32
        )
        total = term if total is None else total + term
    row, col = iotas()
    g00, g01 = total[:TILE, :TILE], total[:TILE, TILE : 2 * TILE]
    g11 = total[TILE:, TILE : 2 * TILE]
    h0, h1 = total[:, 2 * TILE : 3 * TILE], total[:, 3 * TILE :]
    fold = jnp.where(row <= col, g00, g11)
    diag = jnp.sum(jnp.where(row == col, g11, 0.0), axis=0, keepdims=True)
    e_h, e_g = exponent(h0, h1), exponent(g01, fold, diag)
    if scaled:
        by_h, by_g = jnp.exp2(e_h), jnp.exp2(e_g)
        h0, h1, g01, fold, diag = h0 * by_h, h1 * by_h, g01 * by_g, fold * by_g, diag * by_g
    out[: 2 * TILE] = h0
    out[2 * TILE : H_ROWS] = h1
    out[H_ROWS : H_ROWS + TILE] = g01
    out[H_ROWS + TILE : DIAG] = fold
    lines = lax.broadcasted_iota(jnp.int32, (ROWS - DIAG, TILE), 0)
    rest = jnp.where(lines == 0, diag, 0.0)
    rest = jnp.where(lines == H_EXP - DIAG, e_h, rest)
    out[DIAG:] = jnp.where(lines == G_EXP - DIAG, e_g, rest)


def scales(e_h, e_g):
    row = lax.broadcasted_iota(jnp.int32, (1, ROWS, TILE), 1)
    return row, jnp.where(row < H_ROWS, jnp.exp2(e_h), jnp.exp2(e_g))


def exponents(x):
    return x[:, H_EXP : H_EXP + 1], x[:, G_EXP : G_EXP + 1]


def decode(x):
    x = x.astype(F32)
    e_h, e_g = exponents(x)
    return x * scales(-e_h, -e_g)[1], e_h, e_g


def add_on(x, own):
    x, e_h, e_g = decode(x)
    own_h, own_g = exponents(own)
    e_h, e_g = jnp.minimum(e_h, own_h) - 1.0, jnp.minimum(e_g, own_g) - 1.0
    row, scale = scales(e_h, e_g)
    tail = jnp.where(row == H_EXP, e_h, e_g)
    return jnp.where(row <= DIAG, (x + own) * scale, tail).astype(F16)


def split_kernel(chips, ints, out):
    z, c, _ = here()
    near = chips // 2 - 1
    for d in range(1, near + 1):
        to = toward(chips, -d)
        out[2 * d - 2] = ints[2 * to + 1 - c]
        out[2 * d - 1] = ints[2 * to + c]
    out[2 * near] = ints[2 * lax.rem(z + near + 1, chips) + 1 - c]
    out[2 * near + 1] = ints[2 * z + 1 - c]


def chip_rows(chips, ints, other, distance, mine):
    c = here()[1]
    near = chips // 2 - 1
    if distance == 0:
        at = 2 * near + 1
    elif distance > near:
        at = 2 * near
    else:
        at = 2 * distance - 1 - int(mine)
    return [ints[2 * toward(chips, distance) + (c if mine else 1 - c)], other[at]]


def pack_kernel(chips, wanted, ints, other, *outs):
    for group, out in zip(wanted, outs):
        for n, row in enumerate(sum((chip_rows(chips, ints, other, *w) for w in group), [])):
            out[n] = row


def stop_kernel(chips, stop, owners, picks, scaled, ints, other, *rest):
    received, out = rest[:-1], rest[-1]
    for n, mine in enumerate(owners):
        blocks = chip_rows(chips, ints, other, stop, mine)
        for at, ref in picks:
            if at[n] is not None:
                blocks += [received[ref][at[n]], received[ref][at[n] + 1]]
        packed_sum(blocks, out.at[n], scaled)


def final_kernel(occ_at, tiles, mask, occ, virt, sums, amps_t, out):
    row, col = iotas()
    h = jnp.concatenate([sums[: 2 * TILE], sums[2 * TILE : H_ROWS]], axis=1)
    g01 = sums[H_ROWS : H_ROWS + TILE]
    fold = sums[H_ROWS + TILE : DIAG]
    diag = sums[DIAG : DIAG + 8][:1]
    above = jnp.where(row < col, fold, 0.0)
    below = jnp.where(row > col, fold, 0.0)
    g00 = jnp.where(row <= col, fold, 0.0) + above.T
    g11 = below + below.T + jnp.where(row == col, diag, 0.0)
    g = jnp.concatenate(
        [jnp.concatenate([g00, g01], axis=1), jnp.concatenate([g01.T, g11], axis=1)], axis=0
    )
    tt = amps_t[...]
    total = h
    rest = g
    for _ in range(2):
        piece = rest.astype(BF16)
        rest = rest - piece.astype(F32)
        total = total - lax.dot_general(
            piece, tt, (((1,), (1,)), ((), ())), preferred_element_type=F32
        )
        total = total - lax.dot_general(
            tt, piece, (((0,), (0,)), ((), ())), preferred_element_type=F32
        )
    f_sum = occ[occ_at[0]] + occ[occ_at[1]]
    t = tt.astype(F32).T
    e_row = [virt[pl.ds(tiles[s], 1), :] for s in range(2)]
    e_col = [jnp.sum(jnp.where(row == col, e, 0.0), axis=1, keepdims=True) for e in e_row]
    keep = [mask[s].astype(F32) for s in range(2)]
    for a in range(2):
        for b in range(2):
            at = (slice(a * TILE, (a + 1) * TILE), slice(b * TILE, (b + 1) * TILE))
            delta = (e_col[a] + e_row[b]) - f_sum
            out[at] = (keep[a] * keep[b]) * (total[at] + delta * t[at])


def on_device(chips, amplitudes, integrals, pair_occ, dom_tiles, dom_mask, virt_energy, occ_energy):
    naux, wide = integrals.shape[2:]
    far = chips // 2
    vmem = pl.BlockSpec(memory_space=pltpu.VMEM)
    smem = pl.BlockSpec(memory_space=pltpu.SMEM)

    def call(kernel, n_in, shapes, name, small=0):
        return pl.pallas_call(
            kernel,
            in_specs=[smem] * small + [vmem] * n_in,
            out_specs=[vmem] * len(shapes),
            out_shape=[jax.ShapeDtypeStruct(*s) for s in shapes],
            compiler_params=pltpu.CompilerParams(vmem_limit_bytes=8 << 20),
            name=name,
        )

    def permute(x, hops, cross=False):
        pairs = []
        for chip in range(chips):
            for core in range(2):
                to = (chip + (1 - 2 * core) * hops) % chips
                pairs.append((chip * 2 + core, to * 2 + (core ^ int(cross))))
        return lax.ppermute(x, "aux", pairs)

    def pack(wanted, other):
        return call(
            functools.partial(pack_kernel, chips, wanted),
            2,
            [((2 * len(group), naux, wide), BF16) for group in wanted],
            "pack_rows",
        )(ints, other)

    def stop_sums(stop, owners, picks, scaled, other, received):
        return call(
            functools.partial(stop_kernel, chips, stop, owners, picks, scaled),
            2 + len(received),
            [((len(owners), ROWS, TILE), F32)],
            "stop_sums",
        )(ints, other, *received)[0]

    def pairs_at(d):
        return [(d, True)] if d == far else [(d, True), (d, False)]


    ints = integrals[:, 0]
    (other,) = call(
        functools.partial(split_kernel, chips), 1, [((chips, naux, wide), BF16)], "split_cores"
    )(ints)
    other = lax.ppermute(other, "aux", [(i, i ^ 1) for i in range(2 * chips)])

    to_first = list(range(far, FIRST, -1))
    to_second = list(range(FIRST - 1, SECOND, -1))
    to_owner = [(d, n) for d in range(SECOND - 1, 0, -1) for n in range(2)]
    sends = pack([pairs_at(d) for d in to_first], other)
    first_rows = [permute(x, d - FIRST) for d, x in zip(to_first, sends)]
    gate = lax.optimization_barrier((other, *sends))[0]
    sends = pack([pairs_at(d) for d in to_second] + [[(d, n == 0)] for d, n in to_owner], gate)
    second_rows = [permute(x, d - SECOND) for d, x in zip(to_second, sends)]
    owner_rows = [permute(x, d, n == 1) for (d, n), x in zip(to_owner, sends[len(to_second) :])]

    picks = [((0, None) if d == far else (0, 2), at) for at, d in enumerate(to_first)]
    x = stop_sums(FIRST, (True, False), picks, True, other, first_rows).astype(F16)
    x, second_rows, owner_rows = lax.optimization_barrier((x, second_rows, owner_rows))
    moving = permute(x, FIRST - SECOND)

    gate, amplitudes = lax.optimization_barrier((other, amplitudes, x))[:2]
    owned = lax.all_to_all(amplitudes, "pair", split_axis=1, concat_axis=3, tiled=True)

    picks = [((0, 2), at) for at in range(len(to_second))]
    local = stop_sums(SECOND, (True, False), picks, False, gate, second_rows)
    last = [add_on(moving[n : n + 1], local[n : n + 1])[0] for n in range(2)]
    moving = [permute(last[n], SECOND, n == 1) for n in range(2)]

    gate = lax.optimization_barrier((other, last[1]))[0]
    *moving, owned = lax.optimization_barrier((*moving, owned))
    picks = [((0,), at) for at in range(len(owner_rows))]
    local = stop_sums(0, (True,), picks, False, gate, owner_rows)
    sums = (decode(moving[0][None])[0] + decode(moving[1][None])[0] + local)[0]
    amps_t = jnp.swapaxes(owned[0, 0], 0, 1)

    (out,) = call(final_kernel, 3, [((2 * TILE, 2 * TILE), F32)], "residual", 4)(
        pair_occ.reshape(-1),
        dom_tiles.reshape(-1),
        dom_mask.reshape(-1),
        occ_energy,
        virt_energy.reshape(-1, TILE),
        sums,
        amps_t,
    )
    return out[None, None]


def solution(mesh):
    return jax.shard_map(
        functools.partial(on_device, mesh.shape["aux"] // 2),
        mesh=mesh,
        in_specs=(
            P("aux", None, None, "pair"),
            P(None, "pair", "aux", None),
            P("aux", "pair", None),
            P("aux", "pair", None),
            P("aux", "pair", None),
            P(),
            P(),
        ),
        out_specs=P("aux", "pair", None, None),
        check_vma=False,
    )
```

```python
import functools

import jax
import jax.numpy as jnp
from jax import lax
from jax.experimental import pallas as pl
from jax.experimental.pallas import tpu as pltpu
from jax.sharding import PartitionSpec as P

TILE = 128
FIRST, SECOND = 4, 2
H_ROWS, G_ROWS = 4 * TILE, 2 * TILE
DIAG = H_ROWS + G_ROWS
H_EXP, G_EXP = DIAG + 1, DIAG + 2
ROWS = DIAG + 16
F32 = jnp.float32
BF16 = jnp.bfloat16
F16 = jnp.float16


def here():
    me = lax.axis_index("aux")
    c = lax.rem(me, 2)
    return lax.div(me, 2), c, 1 - 2 * c


def toward(chips, distance):
    z, _, way = here()
    return lax.rem(z + way * distance + chips, chips)


def iotas():
    return (
        lax.broadcasted_iota(jnp.int32, (TILE, TILE), 0),
        lax.broadcasted_iota(jnp.int32, (TILE, TILE), 1),
    )


def exponent(*parts):
    top = None
    for part in parts:
        high = jnp.max(jnp.abs(part), axis=0, keepdims=True)
        top = high if top is None else jnp.maximum(top, high)
    top = jnp.max(top, axis=1, keepdims=True)
    power = 14.0 - jnp.floor(jnp.log2(jnp.maximum(top, 1e-30)))
    return jnp.broadcast_to(power, (1, TILE))


def packed_sum(blocks, out, scaled=False):
    total = None
    for block in blocks:
        term = lax.dot_general(
            block[:, : 2 * TILE], block, (((0,), (0,)), ((), ())), preferred_element_type=F32
        )
        total = term if total is None else total + term
    row, col = iotas()
    g00, g01 = total[:TILE, :TILE], total[:TILE, TILE : 2 * TILE]
    g11 = total[TILE:, TILE : 2 * TILE]
    h0, h1 = total[:, 2 * TILE : 3 * TILE], total[:, 3 * TILE :]
    fold = jnp.where(row <= col, g00, g11)
    diag = jnp.sum(jnp.where(row == col, g11, 0.0), axis=0, keepdims=True)
    e_h, e_g = exponent(h0, h1), exponent(g01, fold, diag)
    if scaled:
        by_h, by_g = jnp.exp2(e_h), jnp.exp2(e_g)
        h0, h1, g01, fold, diag = h0 * by_h, h1 * by_h, g01 * by_g, fold * by_g, diag * by_g
    out[: 2 * TILE] = h0
    out[2 * TILE : H_ROWS] = h1
    out[H_ROWS : H_ROWS + TILE] = g01
    out[H_ROWS + TILE : DIAG] = fold
    lines = lax.broadcasted_iota(jnp.int32, (ROWS - DIAG, TILE), 0)
    rest = jnp.where(lines == 0, diag, 0.0)
    rest = jnp.where(lines == H_EXP - DIAG, e_h, rest)
    out[DIAG:] = jnp.where(lines == G_EXP - DIAG, e_g, rest)


def scales(e_h, e_g):
    row = lax.broadcasted_iota(jnp.int32, (1, ROWS, TILE), 1)
    return row, jnp.where(row < H_ROWS, jnp.exp2(e_h), jnp.exp2(e_g))


def exponents(x):
    return x[:, H_EXP : H_EXP + 1], x[:, G_EXP : G_EXP + 1]


def decode(x):
    x = x.astype(F32)
    e_h, e_g = exponents(x)
    return x * scales(-e_h, -e_g)[1], e_h, e_g


def add_on(x, own):
    x, e_h, e_g = decode(x)
    own_h, own_g = exponents(own)
    e_h, e_g = jnp.minimum(e_h, own_h) - 1.0, jnp.minimum(e_g, own_g) - 1.0
    row, scale = scales(e_h, e_g)
    tail = jnp.where(row == H_EXP, e_h, e_g)
    return jnp.where(row <= DIAG, (x + own) * scale, tail).astype(F16)


def split_kernel(chips, ints, out):
    z, c, _ = here()
    near = chips // 2 - 1
    for d in range(1, near + 1):
        to = toward(chips, -d)
        out[2 * d - 2] = ints[2 * to + 1 - c]
        out[2 * d - 1] = ints[2 * to + c]
    out[2 * near] = ints[2 * lax.rem(z + near + 1, chips) + 1 - c]
    out[2 * near + 1] = ints[2 * z + 1 - c]


def chip_rows(chips, ints, other, distance, mine):
    c = here()[1]
    near = chips // 2 - 1
    if distance == 0:
        at = 2 * near + 1
    elif distance > near:
        at = 2 * near
    else:
        at = 2 * distance - 1 - int(mine)
    return [ints[2 * toward(chips, distance) + (c if mine else 1 - c)], other[at]]


def pack_kernel(chips, wanted, ints, other, *outs):
    for group, out in zip(wanted, outs):
        for n, row in enumerate(sum((chip_rows(chips, ints, other, *w) for w in group), [])):
            out[n] = row


def stop_kernel(chips, stop, owners, picks, scaled, ints, other, *rest):
    received, out = rest[:-1], rest[-1]
    for n, mine in enumerate(owners):
        blocks = chip_rows(chips, ints, other, stop, mine)
        for at, ref in picks:
            if at[n] is not None:
                blocks += [received[ref][at[n]], received[ref][at[n] + 1]]
        packed_sum(blocks, out.at[n], scaled)


def final_kernel(occ_at, tiles, mask, occ, virt, sums, amps_t, out):
    row, col = iotas()
    h = jnp.concatenate([sums[: 2 * TILE], sums[2 * TILE : H_ROWS]], axis=1)
    g01 = sums[H_ROWS : H_ROWS + TILE]
    fold = sums[H_ROWS + TILE : DIAG]
    diag = sums[DIAG : DIAG + 8][:1]
    above = jnp.where(row < col, fold, 0.0)
    below = jnp.where(row > col, fold, 0.0)
    g00 = jnp.where(row <= col, fold, 0.0) + above.T
    g11 = below + below.T + jnp.where(row == col, diag, 0.0)
    g = jnp.concatenate(
        [jnp.concatenate([g00, g01], axis=1), jnp.concatenate([g01.T, g11], axis=1)], axis=0
    )
    tt = amps_t[...]
    total = h
    rest = g
    for _ in range(2):
        piece = rest.astype(BF16)
        rest = rest - piece.astype(F32)
        total = total - lax.dot_general(
            piece, tt, (((1,), (1,)), ((), ())), preferred_element_type=F32
        )
        total = total - lax.dot_general(
            tt, piece, (((0,), (0,)), ((), ())), preferred_element_type=F32
        )
    f_sum = occ[occ_at[0]] + occ[occ_at[1]]
    t = tt.astype(F32).T
    e_row = [virt[pl.ds(tiles[s], 1), :] for s in range(2)]
    e_col = [jnp.sum(jnp.where(row == col, e, 0.0), axis=1, keepdims=True) for e in e_row]
    keep = [mask[s].astype(F32) for s in range(2)]
    for a in range(2):
        for b in range(2):
            at = (slice(a * TILE, (a + 1) * TILE), slice(b * TILE, (b + 1) * TILE))
            delta = (e_col[a] + e_row[b]) - f_sum
            out[at] = (keep[a] * keep[b]) * (total[at] + delta * t[at])


def on_device(chips, amplitudes, integrals, pair_occ, dom_tiles, dom_mask, virt_energy, occ_energy):
    naux, wide = integrals.shape[2:]
    far = chips // 2
    vmem = pl.BlockSpec(memory_space=pltpu.VMEM)
    smem = pl.BlockSpec(memory_space=pltpu.SMEM)

    def call(kernel, n_in, shapes, name, small=0):
        return pl.pallas_call(
            kernel,
            in_specs=[smem] * small + [vmem] * n_in,
            out_specs=[vmem] * len(shapes),
            out_shape=[jax.ShapeDtypeStruct(*s) for s in shapes],
            compiler_params=pltpu.CompilerParams(vmem_limit_bytes=8 << 20),
            name=name,
        )

    def permute(x, hops, cross=False):
        pairs = []
        for chip in range(chips):
            for core in range(2):
                to = (chip + (1 - 2 * core) * hops) % chips
                pairs.append((chip * 2 + core, to * 2 + (core ^ int(cross))))
        return lax.ppermute(x, "aux", pairs)

    def pack(wanted, other):
        return call(
            functools.partial(pack_kernel, chips, wanted),
            2,
            [((2 * len(group), naux, wide), BF16) for group in wanted],
            "pack_rows",
        )(ints, other)

    def stop_sums(stop, owners, picks, scaled, other, received):
        return call(
            functools.partial(stop_kernel, chips, stop, owners, picks, scaled),
            2 + len(received),
            [((len(owners), ROWS, TILE), F32)],
            "stop_sums",
        )(ints, other, *received)[0]

    def pairs_at(d):
        return [(d, True)] if d == far else [(d, True), (d, False)]


    ints = integrals[:, 0]
    (other,) = call(
        functools.partial(split_kernel, chips), 1, [((chips, naux, wide), BF16)], "split_cores"
    )(ints)
    other = lax.ppermute(other, "aux", [(i, i ^ 1) for i in range(2 * chips)])

    to_first = list(range(far, FIRST, -1))
    to_second = list(range(FIRST - 1, SECOND, -1))
    to_owner = [(d, n) for d in range(SECOND - 1, 0, -1) for n in range(2)]
    sends = pack([pairs_at(d) for d in to_first], other)
    first_rows = [permute(x, d - FIRST) for d, x in zip(to_first, sends)]
    gate = lax.optimization_barrier((other, *sends))[0]
    sends = pack([pairs_at(d) for d in to_second] + [[(d, n == 0)] for d, n in to_owner], gate)
    second_rows = [permute(x, d - SECOND) for d, x in zip(to_second, sends)]
    owner_rows = [permute(x, d, n == 1) for (d, n), x in zip(to_owner, sends[len(to_second) :])]

    picks = [((0, None) if d == far else (0, 2), at) for at, d in enumerate(to_first)]
    x = stop_sums(FIRST, (True, False), picks, True, other, first_rows).astype(F16)
    x, second_rows, owner_rows = lax.optimization_barrier((x, second_rows, owner_rows))
    moving = permute(x, FIRST - SECOND)

    gate, amplitudes = lax.optimization_barrier((other, amplitudes, x))[:2]
    owned = lax.all_to_all(amplitudes, "pair", split_axis=1, concat_axis=3, tiled=True)

    picks = [((0, 2), at) for at in range(len(to_second))]
    local = stop_sums(SECOND, (True, False), picks, False, gate, second_rows)
    last = [add_on(moving[n : n + 1], local[n : n + 1])[0] for n in range(2)]
    moving = [permute(last[n], SECOND, n == 1) for n in range(2)]

    gate = lax.optimization_barrier((other, last[1]))[0]
    gate, owned = lax.optimization_barrier((gate, owned))
    picks = [((0,), at) for at in range(len(owner_rows))]
    local = stop_sums(0, (True,), picks, False, gate, owner_rows)
    sums = (decode(moving[0][None])[0] + decode(moving[1][None])[0] + local)[0]
    amps_t = jnp.swapaxes(owned[0, 0], 0, 1)

    (out,) = call(final_kernel, 3, [((2 * TILE, 2 * TILE), F32)], "residual", 4)(
        pair_occ.reshape(-1),
        dom_tiles.reshape(-1),
        dom_mask.reshape(-1),
        occ_energy,
        virt_energy.reshape(-1, TILE),
        sums,
        amps_t,
    )
    return out[None, None]


def solution(mesh):
    return jax.shard_map(
        functools.partial(on_device, mesh.shape["aux"] // 2),
        mesh=mesh,
        in_specs=(
            P("aux", None, None, "pair"),
            P(None, "pair", "aux", None),
            P("aux", "pair", None),
            P("aux", "pair", None),
            P("aux", "pair", None),
            P(),
            P(),
        ),
        out_specs=P("aux", "pair", None, None),
        check_vma=False,
    )
```

```python
import functools

import jax
import jax.numpy as jnp
from jax import lax
from jax.experimental import pallas as pl
from jax.experimental.pallas import tpu as pltpu
from jax.sharding import PartitionSpec as P

TILE = 128
FIRST, SECOND = 4, 2
H_ROWS, G_ROWS = 4 * TILE, 2 * TILE
DIAG = H_ROWS + G_ROWS
H_EXP, G_EXP = DIAG + 1, DIAG + 2
ROWS = DIAG + 16
F32 = jnp.float32
BF16 = jnp.bfloat16
F16 = jnp.float16


def here():
    me = lax.axis_index("aux")
    c = lax.rem(me, 2)
    return lax.div(me, 2), c, 1 - 2 * c


def toward(chips, distance):
    z, _, way = here()
    return lax.rem(z + way * distance + chips, chips)


def iotas():
    return (
        lax.broadcasted_iota(jnp.int32, (TILE, TILE), 0),
        lax.broadcasted_iota(jnp.int32, (TILE, TILE), 1),
    )


def exponent(*parts):
    top = None
    for part in parts:
        high = jnp.max(jnp.abs(part), axis=0, keepdims=True)
        top = high if top is None else jnp.maximum(top, high)
    top = jnp.max(top, axis=1, keepdims=True)
    power = 14.0 - jnp.floor(jnp.log2(jnp.maximum(top, 1e-30)))
    return jnp.broadcast_to(power, (1, TILE))


def packed_sum(blocks, out, scaled=False):
    total = None
    for block in blocks:
        term = lax.dot_general(
            block[:, : 2 * TILE], block, (((0,), (0,)), ((), ())), preferred_element_type=F32
        )
        total = term if total is None else total + term
    row, col = iotas()
    g00, g01 = total[:TILE, :TILE], total[:TILE, TILE : 2 * TILE]
    g11 = total[TILE:, TILE : 2 * TILE]
    h0, h1 = total[:, 2 * TILE : 3 * TILE], total[:, 3 * TILE :]
    fold = jnp.where(row <= col, g00, g11)
    diag = jnp.sum(jnp.where(row == col, g11, 0.0), axis=0, keepdims=True)
    e_h, e_g = exponent(h0, h1), exponent(g01, fold, diag)
    if scaled:
        by_h, by_g = jnp.exp2(e_h), jnp.exp2(e_g)
        h0, h1, g01, fold, diag = h0 * by_h, h1 * by_h, g01 * by_g, fold * by_g, diag * by_g
    out[: 2 * TILE] = h0
    out[2 * TILE : H_ROWS] = h1
    out[H_ROWS : H_ROWS + TILE] = g01
    out[H_ROWS + TILE : DIAG] = fold
    lines = lax.broadcasted_iota(jnp.int32, (ROWS - DIAG, TILE), 0)
    rest = jnp.where(lines == 0, diag, 0.0)
    rest = jnp.where(lines == H_EXP - DIAG, e_h, rest)
    out[DIAG:] = jnp.where(lines == G_EXP - DIAG, e_g, rest)


def scales(e_h, e_g):
    row = lax.broadcasted_iota(jnp.int32, (1, ROWS, TILE), 1)
    return row, jnp.where(row < H_ROWS, jnp.exp2(e_h), jnp.exp2(e_g))


def exponents(x):
    return x[:, H_EXP : H_EXP + 1], x[:, G_EXP : G_EXP + 1]


def decode(x):
    x = x.astype(F32)
    e_h, e_g = exponents(x)
    return x * scales(-e_h, -e_g)[1], e_h, e_g


def add_on(x, own):
    x, e_h, e_g = decode(x)
    own_h, own_g = exponents(own)
    e_h, e_g = jnp.minimum(e_h, own_h) - 1.0, jnp.minimum(e_g, own_g) - 1.0
    row, scale = scales(e_h, e_g)
    tail = jnp.where(row == H_EXP, e_h, e_g)
    return jnp.where(row <= DIAG, (x + own) * scale, tail).astype(F16)


def split_kernel(chips, ints, out):
    z, c, _ = here()
    near = chips // 2 - 1
    for d in range(1, near + 1):
        to = toward(chips, -d)
        out[2 * d - 2] = ints[2 * to + 1 - c]
        out[2 * d - 1] = ints[2 * to + c]
    out[2 * near] = ints[2 * lax.rem(z + near + 1, chips) + 1 - c]
    out[2 * near + 1] = ints[2 * z + 1 - c]


def chip_rows(chips, ints, other, distance, mine):
    c = here()[1]
    near = chips // 2 - 1
    if distance == 0:
        at = 2 * near + 1
    elif distance > near:
        at = 2 * near
    else:
        at = 2 * distance - 1 - int(mine)
    return [ints[2 * toward(chips, distance) + (c if mine else 1 - c)], other[at]]


def pack_kernel(chips, wanted, ints, other, *outs):
    for group, out in zip(wanted, outs):
        for n, row in enumerate(sum((chip_rows(chips, ints, other, *w) for w in group), [])):
            out[n] = row


def stop_kernel(chips, stop, owners, picks, scaled, ints, other, *rest):
    received, out = rest[:-1], rest[-1]
    for n, mine in enumerate(owners):
        blocks = chip_rows(chips, ints, other, stop, mine)
        for at, ref in picks:
            if at[n] is not None:
                blocks += [received[ref][at[n]], received[ref][at[n] + 1]]
        packed_sum(blocks, out.at[n], scaled)


def final_kernel(occ_at, tiles, mask, occ, virt, sums, amps_t, out):
    row, col = iotas()
    h = jnp.concatenate([sums[: 2 * TILE], sums[2 * TILE : H_ROWS]], axis=1)
    g01 = sums[H_ROWS : H_ROWS + TILE]
    fold = sums[H_ROWS + TILE : DIAG]
    diag = sums[DIAG : DIAG + 8][:1]
    above = jnp.where(row < col, fold, 0.0)
    below = jnp.where(row > col, fold, 0.0)
    g00 = jnp.where(row <= col, fold, 0.0) + above.T
    g11 = below + below.T + jnp.where(row == col, diag, 0.0)
    g = jnp.concatenate(
        [jnp.concatenate([g00, g01], axis=1), jnp.concatenate([g01.T, g11], axis=1)], axis=0
    )
    tt = amps_t[...]
    total = h
    rest = g
    for _ in range(2):
        piece = rest.astype(BF16)
        rest = rest - piece.astype(F32)
        total = total - lax.dot_general(
            piece, tt, (((1,), (1,)), ((), ())), preferred_element_type=F32
        )
        total = total - lax.dot_general(
            tt, piece, (((0,), (0,)), ((), ())), preferred_element_type=F32
        )
    f_sum = occ[occ_at[0]] + occ[occ_at[1]]
    t = tt.astype(F32).T
    e_row = [virt[pl.ds(tiles[s], 1), :] for s in range(2)]
    e_col = [jnp.sum(jnp.where(row == col, e, 0.0), axis=1, keepdims=True) for e in e_row]
    keep = [mask[s].astype(F32) for s in range(2)]
    for a in range(2):
        for b in range(2):
            at = (slice(a * TILE, (a + 1) * TILE), slice(b * TILE, (b + 1) * TILE))
            delta = (e_col[a] + e_row[b]) - f_sum
            out[at] = (keep[a] * keep[b]) * (total[at] + delta * t[at])


def on_device(chips, amplitudes, integrals, pair_occ, dom_tiles, dom_mask, virt_energy, occ_energy):
    naux, wide = integrals.shape[2:]
    far = chips // 2
    vmem = pl.BlockSpec(memory_space=pltpu.VMEM)
    smem = pl.BlockSpec(memory_space=pltpu.SMEM)

    def call(kernel, n_in, shapes, name, small=0):
        return pl.pallas_call(
            kernel,
            in_specs=[smem] * small + [vmem] * n_in,
            out_specs=[vmem] * len(shapes),
            out_shape=[jax.ShapeDtypeStruct(*s) for s in shapes],
            compiler_params=pltpu.CompilerParams(vmem_limit_bytes=8 << 20),
            name=name,
        )

    def permute(x, hops, cross=False):
        pairs = []
        for chip in range(chips):
            for core in range(2):
                to = (chip + (1 - 2 * core) * hops) % chips
                pairs.append((chip * 2 + core, to * 2 + (core ^ int(cross))))
        return lax.ppermute(x, "aux", pairs)

    def pack(wanted, other):
        return call(
            functools.partial(pack_kernel, chips, wanted),
            2,
            [((2 * len(group), naux, wide), BF16) for group in wanted],
            "pack_rows",
        )(ints, other)

    def stop_sums(stop, owners, picks, scaled, other, received):
        return call(
            functools.partial(stop_kernel, chips, stop, owners, picks, scaled),
            2 + len(received),
            [((len(owners), ROWS, TILE), F32)],
            "stop_sums",
        )(ints, other, *received)[0]

    def pairs_at(d):
        return [(d, True)] if d == far else [(d, True), (d, False)]


    ints = integrals[:, 0]
    (other,) = call(
        functools.partial(split_kernel, chips), 1, [((chips, naux, wide), BF16)], "split_cores"
    )(ints)
    other = lax.ppermute(other, "aux", [(i, i ^ 1) for i in range(2 * chips)])

    to_first = list(range(far, FIRST, -1))
    to_second = list(range(FIRST - 1, SECOND, -1))
    to_owner = [(d, n) for d in range(SECOND - 1, 0, -1) for n in range(2)]
    sends = pack([pairs_at(d) for d in to_first], other)
    first_rows = [permute(x, d - FIRST) for d, x in zip(to_first, sends)]
    gate = lax.optimization_barrier((other, *sends))[0]
    sends = pack([pairs_at(d) for d in to_second] + [[(d, n == 0)] for d, n in to_owner], gate)
    second_rows = [permute(x, d - SECOND) for d, x in zip(to_second, sends)]
    owner_rows = [permute(x, d, n == 1) for (d, n), x in zip(to_owner, sends[len(to_second) :])]

    picks = [((0, None) if d == far else (0, 2), at) for at, d in enumerate(to_first)]
    x = stop_sums(FIRST, (True, False), picks, True, other, first_rows).astype(F16)
    x, second_rows, owner_rows = lax.optimization_barrier((x, second_rows, owner_rows))
    moving = permute(x, FIRST - SECOND)

    gate = lax.optimization_barrier((other, x))[0]
    picks = [((0, 2), at) for at in range(len(to_second))]
    local = stop_sums(SECOND, (True, False), picks, False, gate, second_rows)
    amplitudes = lax.optimization_barrier((amplitudes, local))[0]
    owned = lax.all_to_all(amplitudes, "pair", split_axis=1, concat_axis=3, tiled=True)
    last = [add_on(moving[n : n + 1], local[n : n + 1])[0] for n in range(2)]
    moving = [permute(last[n], SECOND, n == 1) for n in range(2)]

    gate = lax.optimization_barrier((other, last[1]))[0]
    gate, owned = lax.optimization_barrier((gate, owned))
    picks = [((0,), at) for at in range(len(owner_rows))]
    local = stop_sums(0, (True,), picks, False, gate, owner_rows)
    sums = (decode(moving[0][None])[0] + decode(moving[1][None])[0] + local)[0]
    amps_t = jnp.swapaxes(owned[0, 0], 0, 1)

    (out,) = call(final_kernel, 3, [((2 * TILE, 2 * TILE), F32)], "residual", 4)(
        pair_occ.reshape(-1),
        dom_tiles.reshape(-1),
        dom_mask.reshape(-1),
        occ_energy,
        virt_energy.reshape(-1, TILE),
        sums,
        amps_t,
    )
    return out[None, None]


def solution(mesh):
    return jax.shard_map(
        functools.partial(on_device, mesh.shape["aux"] // 2),
        mesh=mesh,
        in_specs=(
            P("aux", None, None, "pair"),
            P(None, "pair", "aux", None),
            P("aux", "pair", None),
            P("aux", "pair", None),
            P("aux", "pair", None),
            P(),
            P(),
        ),
        out_specs=P("aux", "pair", None, None),
        check_vma=False,
    )
```
